32 devices in a mesh: head: 4 (over x, core), blk: 8 (over z, y).
Axes of the slice: x: 2, y: 2, z: 4, core: 2. Of those that a mesh axis runs over, the one named last changes fastest.
Arguments:
- queries: bfloat16 [4096, 24, 128], P(('head', 'blk')), may hold values from -5 to 5
- keys: bfloat16 [4096, 24, 128], P(('head', 'blk')), may hold values from -4 to 4
- values: bfloat16 [4096, 24, 128], P(('head', 'blk')), may hold values from -6 to 6
- block_mask: int32 [24, 32, 32], replicated, may hold values from 0 to 1, as said below
- out_weight: bfloat16 [3072, 3072], replicated, may hold values from -0.109375 to 0.109375
Outputs:
- projected: bfloat16 [4096, 3072], P(('head', 'blk'))
The draws below stay inside these ranges and needn't reach their ends.
Inputs may be any that keep to these rules, and one draw needn't show every extreme that they name: Every diagonal entry block_mask[h, b, b] is 1; other entries are 0 or 1.
All inputs are finite; a program needn't handle non-finite values.
Results may differ from the reference program's by a relative error of at most 0.008.
Values may be sent and summed in bfloat16 or wider, within the bound.
No kernel may reach another device: no remote copies, remote signals or barrier semaphores. Data moves between devices by JAX's collectives and lax.ppermute only.
A program may use at most 128 MiB of HBM per device.

```python
import jax
import jax.numpy as jnp
from jax import lax

D = 3072
HEADS = 24
HD = 128
BLOCK = 128
TOKENS = 4096


def draw_queries(key, part):
    base = jnp.clip(jax.random.normal(jax.random.fold_in(key, 1), (TOKENS, HEADS, HD), jnp.float32), -4.0, 4.0)
    return base.astype(jnp.bfloat16)


def draw_keys(key, part):
    base = jnp.clip(jax.random.normal(jax.random.fold_in(key, 2), (TOKENS, HEADS, HD), jnp.float32), -4.0, 4.0)
    return base.astype(jnp.bfloat16)


def draw_block_mask(key, part):
    count = TOKENS // BLOCK
    powers = jax.random.randint(jax.random.fold_in(key, 3), (HEADS,), 0, 5)
    widths = jnp.left_shift(jnp.ones((HEADS,), jnp.int32), powers.astype(jnp.int32))
    shuffled = jax.random.permutation(jax.random.fold_in(key, 5), HEADS).astype(jnp.int32)
    temporal = (shuffled % 2 == 0)[:, None, None]
    divisors = jnp.left_shift(jnp.ones((HEADS,), jnp.int32), jax.random.randint(jax.random.fold_in(key, 6), (HEADS,), 2, 5).astype(jnp.int32))
    periods = jnp.maximum(count // divisors, 2)[:, None, None]
    spread = jax.random.randint(jax.random.fold_in(key, 8), (HEADS,), 0, 2)[:, None, None]
    qpos = jnp.arange(count, dtype=jnp.int32)[:, None]
    kpos = jnp.arange(count, dtype=jnp.int32)[None, :]
    dist = jnp.abs(qpos - kpos)[None, :, :]
    band = dist <= widths[:, None, None]
    phase = dist % periods
    stripe = jnp.minimum(phase, periods - phase) <= spread
    pattern = jnp.where(temporal, stripe, band)
    keep = jax.random.randint(jax.random.fold_in(key, 4), (HEADS, count, count), 0, 4) > 0
    diagonal = (qpos == kpos)[None, :, :]
    return (pattern & keep | diagonal).astype(jnp.int32)


def shard_levels(stream_key, shape, cuts, low, largest):
    factor_of, own = 1.0, jax.random.fold_in(stream_key, 6)
    for position, parts in cuts:
        draws = jnp.exp(jax.random.uniform(jax.random.fold_in(own, position), (parts,), jnp.float32, low / len(cuts), largest / len(cuts)))
        factor_of = factor_of * jnp.repeat(draws, shape[position] // parts).reshape([-1 if axis == position else 1 for axis in range(len(shape))])
    return factor_of


def noise(rng, shape, width, reach, cuts=(), held_as=jnp.bfloat16):
    result = width * jax.random.normal(rng, shape, jnp.float32)
    if cuts:
        result = result * shard_levels(rng, shape, cuts, -0.22, 0.18)
    return jnp.clip(result, -reach, reach).astype(held_as)


def setup_inputs(seed: int = 0) -> dict:
    streams_of = jax.random.split(jax.random.key(seed), 6)
    queries = draw_queries(jax.random.fold_in(streams_of[5], 71), 0)
    keys = draw_keys(jax.random.fold_in(streams_of[5], 71), 0)
    values = noise(streams_of[2], (TOKENS, HEADS, HD), 1.0, 6.0, ((0, 32),))
    block_mask = draw_block_mask(jax.random.fold_in(streams_of[5], 71), 0)
    out_weight = noise(streams_of[4], (HEADS * HD, D), (HEADS * HD) ** -0.5, 0.109375)
    return dict(queries=queries, keys=keys, values=values, block_mask=block_mask, out_weight=out_weight)


def reference(queries, keys, values, block_mask, out_weight):
    tokens, heads, hdim = queries.shape
    qrows = 8 * BLOCK
    nblocks = tokens // BLOCK
    scale = hdim ** -0.5

    def one_head(group):
        qh, kh, vh, mh = group

        def one_rows(index):
            start = (index * qrows).astype(jnp.int32)
            rows_q = lax.dynamic_slice_in_dim(qh, start, qrows, 0)
            scores = jnp.dot(rows_q, kh.T, preferred_element_type=jnp.float32) * scale
            mrows = lax.dynamic_slice_in_dim(mh, (index * 8).astype(jnp.int32), 8, 0)
            allowed = (mrows > 0)[:, None, :, None]
            grid = scores.reshape(8, BLOCK, nblocks, BLOCK)
            top = jnp.max(jnp.where(allowed, grid, -1e30), axis=(2, 3), keepdims=True)
            expo = jnp.where(allowed, jnp.exp(grid - top), 0.0)
            total = jnp.sum(expo, axis=(2, 3)).reshape(qrows, 1)
            weights = expo.reshape(qrows, tokens).astype(jnp.bfloat16)
            summed = jnp.dot(weights, vh, preferred_element_type=jnp.float32)
            return (summed / total).astype(jnp.bfloat16)

        blocks = lax.map(one_rows, jnp.arange(tokens // qrows, dtype=jnp.int32))
        return blocks.reshape(tokens, hdim)

    stacked = (jnp.transpose(queries, (1, 0, 2)), jnp.transpose(keys, (1, 0, 2)),
               jnp.transpose(values, (1, 0, 2)), block_mask)
    attended = lax.map(one_head, stacked)
    flat = jnp.transpose(attended, (1, 0, 2)).reshape(tokens, heads * hdim)
    return jnp.dot(flat, out_weight, preferred_element_type=jnp.float32).astype(jnp.bfloat16)
```

```python
import functools
import math

import jax
import jax.numpy as jnp
import numpy as np
from jax import lax
from jax.experimental import pallas as pl
from jax.experimental.pallas import tpu as pltpu
from jax.sharding import Mesh
from jax.sharding import PartitionSpec as P

BLOCK = 128
NEG = -1e30
CORES = 2
PLANES = 4


def swap(size, bit):
    return [(i, i ^ bit) for i in range(size)]


def attend_kernel(picks, widths, rows, scale, first, last, *refs):
    bias_ref, q_ref = refs[:2]
    kv_refs = refs[2 : 2 + len(widths)]
    rest = refs[2 + len(widths) :]
    if not first:
        m_in, acc_in = rest[:2]
        rest = rest[2:]
    groups, _, block, hdim = q_ref.shape
    qb = rows // block

    def tile(index, carry):
        q = q_ref[pl.ds(index * qb, qb), 0].reshape(rows, hdim)
        if first:
            m = jnp.full((rows, 1), NEG, jnp.float32)
            acc = jnp.zeros((rows, 2 * hdim), jnp.float32)
        else:
            m = m_in[pl.ds(index * rows, rows), :1]
            acc = acc_in[pl.ds(index * rows, rows), :]
        for number, (which, kpart, vpart) in enumerate(picks):
            ref = kv_refs[which]
            span = ref.shape[0] * block
            k = ref[:, kpart].reshape(span, hdim)
            v = ref[:, vpart].reshape(span, hdim)
            v = jnp.concatenate([v, jnp.ones((span, hdim), v.dtype)], axis=1)
            s = lax.dot_general(q, k, (((1,), (1,)), ((), ())), preferred_element_type=jnp.float32)
            bias = bias_ref[pl.ds(index * qb, qb), :, number * span : (number + 1) * span]
            s = (s.reshape(qb, block, span) * scale + bias).reshape(rows, span)
            m_next = jnp.maximum(m, jnp.max(s, axis=1, keepdims=True))
            p = jnp.exp2(s - m_next).astype(jnp.bfloat16)
            acc = acc * jnp.exp2(m - m_next) + jnp.dot(p, v, preferred_element_type=jnp.float32)
            m = m_next
        if last:
            out = (acc[:, :hdim] / acc[:, hdim:]).astype(jnp.bfloat16)
            rest[0][pl.ds(index * qb, qb)] = out.reshape(qb, block, hdim)
        else:
            rest[0][pl.ds(index * rows, rows), :] = jnp.broadcast_to(m, (rows, hdim))
            rest[1][pl.ds(index * rows, rows), :] = acc
        return carry

    lax.fori_loop(0, groups // qb, tile, 0)


def attend(bias, q, arrays, picks, state, last):
    groups, _, block, hdim = q.shape
    rows = 2 * block if groups % 2 == 0 else block
    total = groups * block
    first = state is None
    widths = [a.shape[0] * block for a in arrays]
    vmem = pl.BlockSpec(memory_space=pltpu.VMEM)
    if last:
        out_shape = jax.ShapeDtypeStruct((groups, block, hdim), jnp.bfloat16)
        out_specs = vmem
    else:
        out_shape = (
            jax.ShapeDtypeStruct((total, hdim), jnp.float32),
            jax.ShapeDtypeStruct((total, 2 * hdim), jnp.float32),
        )
        out_specs = (vmem, vmem)
    args = [bias, q, *arrays, *(() if first else state)]
    scale = hdim**-0.5 * math.log2(math.e)
    keys = sum(widths[w] for w, _, _ in picks)
    return pl.pallas_call(
        functools.partial(attend_kernel, picks, widths, rows, scale, first, last),
        out_shape=out_shape,
        in_specs=[vmem] * len(args),
        out_specs=out_specs,
        compiler_params=pltpu.CompilerParams(vmem_limit_bytes=40 * 1024 * 1024),
        cost_estimate=pl.CostEstimate(
            flops=4 * total * keys * hdim, bytes_accessed=4 * keys * hdim, transcendentals=total * keys
        ),
    )(*args)


def shards(split, gather, queries, keys, values, block_mask, out_weight):
    sizes = {a: lax.axis_size(a) for a in ("x", "c", "zh", "zl", "y")}
    n_split = math.prod(sizes[a] for a in split)
    tok, heads, hdim = queries.shape
    chunks = heads // n_split
    width = n_split * hdim
    cols = out_weight.shape[1]

    grid = tuple(sizes.values())
    mask = block_mask.reshape((chunks, n_split) + grid + grid)
    mask = lax.dynamic_index_in_dim(mask, lax.axis_index(split), 1, keepdims=False)
    names = list(sizes)
    for a in ("c", "zh") + gather:
        mask = lax.dynamic_index_in_dim(mask, lax.axis_index(a), 1 + names.index(a), keepdims=True)
    mask = mask.reshape((chunks, n_split) + grid)
    order = ("zh",) + gather + ("c",)
    pieces = [mask]
    for a in order:
        d = 2 + names.index(a)
        here = lax.axis_index(a)
        pieces = [
            lax.dynamic_index_in_dim(p, here ^ bit, d, keepdims=True) for bit in range(sizes[a]) for p in pieces
        ]
    mask = jnp.stack([p.reshape(chunks, n_split, n_split) for p in pieces], axis=2)
    mask = mask.reshape(chunks, n_split, 1, -1)
    bias = jnp.repeat(jnp.where(mask > 0, 0.0, NEG).astype(jnp.float32), BLOCK, axis=3)

    def across(a, axis, bit):
        return lax.ppermute(a, axis, swap(sizes[axis], bit))

    def spread(a):
        return lax.all_to_all(a, split, split_axis=0, concat_axis=0, tiled=True)

    def chunk(a, j):
        return jnp.transpose(a[:, j * n_split : (j + 1) * n_split], (1, 0, 2))

    def gathered(arrays, axes):
        for a in axes:
            arrays = [
                p if bit == 0 else across(p, a, bit) for bit in range(sizes[a]) for p in arrays
            ]
        return arrays

    far = across(jnp.stack([chunk(keys, 0), chunk(values, 0)], axis=1), "zh", 1)
    outs = []
    states = []
    for j in range(1, chunks):
        own = jnp.stack([chunk(queries, j), chunk(keys, j), chunk(values, j)], axis=1)
        got = spread(own)
        q, near = got[:, :1], got[:, 1:]
        states.append((q, near, across(near, "zh", 1)))
    own = jnp.stack([chunk(queries, 0), chunk(keys, 0), chunk(values, 0)], axis=1)
    got = spread(jnp.concatenate([own, far], axis=1))
    arrays = gathered([got[:, 1:]], gather + ("c",))
    half = len(arrays)
    picks = []
    for number in range(2 * half):
        which, side = number // 2, number % 2
        picks.append((which, 2 * side, 2 * side + 1))
    outs.append(attend(bias[0], got[:, :1], arrays, tuple(picks), None, True))
    for j, (q, near, far) in enumerate(states, 1):
        near_all = gathered([near], gather + ("c",))
        far_all = gathered([far], gather + ("c",))
        b = bias[j].reshape(n_split, 1, half, 2, -1)
        near_bias = b[:, :, :, 0].reshape(n_split, 1, -1)
        far_bias = b[:, :, :, 1].reshape(n_split, 1, -1)
        pick = tuple((i, 0, 1) for i in range(half))
        state = attend(near_bias, q, near_all, pick, None, False)
        outs.append(attend(far_bias, q, far_all, pick, state, True))

    def project(part, j):
        flat = jnp.transpose(part, (1, 0, 2)).reshape(tok, width)
        rows = out_weight[j * width : (j + 1) * width]
        return jnp.dot(flat, rows, preferred_element_type=jnp.float32)

    early = spread(jnp.stack(outs[:-1], axis=1))
    total = sum(project(early[:, j], j) for j in range(chunks - 1))
    late = spread(outs[-1])
    return (total + project(late, chunks - 1)).astype(jnp.bfloat16)


def solution(mesh):
    n_head, n_blk = mesh.shape["head"], mesh.shape["blk"]
    x, y = n_head // CORES, n_blk // PLANES
    shape = (x, CORES, 2, PLANES // 2, y)
    wide = Mesh(np.asarray(mesh.devices).reshape(shape), ("x", "c", "zh", "zl", "y"))
    split, gather = (("x", "zl", "y"), ()) if x * y * 2 <= 8 else (("x", "zl"), ("y",))
    every = ("x", "c", "zh", "zl", "y")
    spec = P(every, None, None)
    return jax.shard_map(
        functools.partial(shards, split, gather),
        mesh=wide,
        in_specs=(spec, spec, spec, P(), P()),
        out_specs=P(every, None),
        check_vma=False,
    )
```

```python
import functools
import math

import jax
import jax.numpy as jnp
import numpy as np
from jax import lax
from jax.experimental import pallas as pl
from jax.experimental.pallas import tpu as pltpu
from jax.sharding import Mesh
from jax.sharding import PartitionSpec as P

BLOCK = 128
NEG = -1e30
CORES = 2
PLANES = 4
AXES = ("x", "c", "zh", "zl", "y")
VMEM = pl.BlockSpec(memory_space=pltpu.VMEM)
SMEM = pl.BlockSpec(memory_space=pltpu.SMEM)
PARAMS = pltpu.CompilerParams(vmem_limit_bytes=40 * 1024 * 1024)


def swap(size, bit):
    return [(i, i ^ bit) for i in range(size)]


def after(value, *others):
    return lax.optimization_barrier((value, *others))[0]


def bias_kernel(sources, place_ref, mask_ref, rows_ref, cols_ref, bias_ref):
    chunks, tiles, qb, _ = bias_ref.shape
    blocks = mask_ref.shape[1]
    span = cols_ref.shape[1]
    groups = tiles * qb
    group = place_ref[sources]
    lanes = lax.broadcasted_iota(jnp.int32, (groups, blocks), 1)
    mine = (lanes == rows_ref[...] + place_ref[0]).astype(jnp.bfloat16)
    rows = []
    for j in range(chunks):
        mask = (mask_ref[j * groups + group] > 0).astype(jnp.bfloat16)
        rows.append(jnp.dot(mine, mask, preferred_element_type=jnp.float32))
    rows = jnp.concatenate(rows, axis=0).astype(jnp.bfloat16)
    depth = lax.broadcasted_iota(jnp.int32, (blocks, span), 0)
    for n in range(sources):
        pick = (depth == cols_ref[...] + place_ref[n]).astype(jnp.bfloat16)
        seen = jnp.dot(rows, pick, preferred_element_type=jnp.float32)
        bias = jnp.where(seen > 0.5, 0.0, NEG)
        bias_ref[:, :, :, n * span : (n + 1) * span] = bias.reshape(chunks, tiles, qb, span)


def attend_kernel(picks, count, chunk, sub, scale, first, last, *refs):
    bias_ref, q_ref = refs[:2]
    kv_refs = refs[2 : 2 + count]
    rest = refs[2 + count :]
    if not first:
        m_in, acc_in = rest[:2]
        rest = rest[2:]
    _, tiles, qb, _ = bias_ref.shape
    block, hdim = q_ref.shape[2:]
    rows = qb * block

    def tile(index, carry):
        q = q_ref[pl.ds(index * qb, qb), 0].reshape(rows, hdim)
        if first:
            m = jnp.full((rows, 1), NEG, jnp.float32)
            acc = jnp.zeros((rows, 2 * hdim), jnp.float32)
        else:
            m = m_in[pl.ds(index * rows, rows), :1]
            acc = acc_in[pl.ds(index * rows, rows), :]
        for kref, kpart, vref, vpart, source in picks:
            span = kv_refs[kref].shape[0] * block
            for start in range(0, span, sub):
                some = slice(start // block, (start + sub) // block)
                k = kv_refs[kref][some, kpart].reshape(sub, hdim)
                v = kv_refs[vref][some, vpart].reshape(sub, hdim)
                v = jnp.concatenate([v, jnp.ones((sub, hdim), v.dtype)], axis=1)
                s = lax.dot_general(q, k, (((1,), (1,)), ((), ())), preferred_element_type=jnp.float32)
                at = source * span + start
                bias = bias_ref[chunk, index, :, at : at + sub]
                s = (s.reshape(qb, block, sub) * scale + bias[:, None, :]).reshape(rows, sub)
                m_next = jnp.maximum(m, jnp.max(s, axis=1, keepdims=True))
                p = jnp.exp2(s - m_next).astype(jnp.bfloat16)
                acc = acc * jnp.exp2(m - m_next) + jnp.dot(p, v, preferred_element_type=jnp.float32)
                m = m_next
        if last:
            out = (acc[:, :hdim] / acc[:, hdim:]).astype(jnp.bfloat16)
            rest[0][pl.ds(index * qb, qb)] = out.reshape(qb, block, hdim)
        else:
            rest[0][pl.ds(index * rows, rows), :] = jnp.broadcast_to(m, (rows, hdim))
            rest[1][pl.ds(index * rows, rows), :] = acc
        return carry

    lax.fori_loop(0, tiles, tile, 0)


def attend(bias, chunk, q, arrays, picks, state, last):
    groups, _, block, hdim = q.shape
    total = groups * block
    first = state is None
    if last:
        out_shape = jax.ShapeDtypeStruct((groups, block, hdim), jnp.bfloat16)
        out_specs = VMEM
    else:
        out_shape = (
            jax.ShapeDtypeStruct((total, hdim), jnp.float32),
            jax.ShapeDtypeStruct((total, 2 * hdim), jnp.float32),
        )
        out_specs = (VMEM, VMEM)
    args = [bias, q, *arrays, *(() if first else state)]
    scale = hdim**-0.5 * math.log2(math.e)
    keys = len(picks) * total
    sub = min(4, groups) * block
    return pl.pallas_call(
        functools.partial(attend_kernel, picks, len(arrays), chunk, sub, scale, first, last),
        out_shape=out_shape,
        in_specs=[VMEM] * len(args),
        out_specs=out_specs,
        compiler_params=PARAMS,
        cost_estimate=pl.CostEstimate(
            flops=total, bytes_accessed=4 * keys, transcendentals=0
        ),
    )(*args)


def shards(split, gather, queries, keys, values, block_mask, out_weight):
    sizes = {a: lax.axis_size(a) for a in AXES}
    stride = {a: math.prod(list(sizes.values())[i + 1 :]) for i, a in enumerate(AXES)}
    n_split = math.prod(sizes[a] for a in split)
    tok, heads, hdim = queries.shape
    chunks = heads // n_split
    width = n_split * hdim

    order = ("zh",) + gather + ("c",)
    bits = [dict(zip(reversed(order), b)) for b in np.ndindex(*(sizes[a] for a in reversed(order)))]
    sources = len(bits)
    half = sources // 2
    place = sum(
        (lax.axis_index(a) ^ np.array([b[a] for b in bits] + [0], np.int32)) * stride[a] for a in order
    )
    place = jnp.where(np.arange(sources + 1) == sources, lax.axis_index(split), place).astype(jnp.int32)
    local = np.zeros(1, np.int32)
    for a in split:
        local = (local[:, None] + np.arange(sizes[a], dtype=np.int32) * stride[a]).reshape(-1)
    qb = min(4, n_split)

    def across(a, axis, bit):
        return lax.ppermute(a, axis, swap(sizes[axis], bit))

    def spread(a):
        return lax.all_to_all(a, split, split_axis=0, concat_axis=0, tiled=True)

    def chunk(a, j):
        return jnp.transpose(a[:, j * n_split : (j + 1) * n_split], (1, 0, 2))

    def gathered(array, axes):
        arrays = [array]
        for a in axes:
            arrays = [p if bit == 0 else across(p, a, bit) for bit in range(sizes[a]) for p in arrays]
        return arrays

    first = jnp.stack([chunk(keys, 0), chunk(values, 0)], axis=1)
    far0 = across(first, "zh", 1)
    keys1, queries1, values1 = after((keys, queries, values), first)
    own = [jnp.stack([chunk(a, j) for a in (queries1, keys1, values1)], axis=1) for j in range(chunks)]
    own = [after(o, own[1]) if j != 1 else o for j, o in enumerate(own)]
    bias = pl.pallas_call(
        functools.partial(bias_kernel, sources),
        out_shape=jax.ShapeDtypeStruct((chunks, n_split // qb, qb, sources * n_split * BLOCK), jnp.float32),
        in_specs=[SMEM, VMEM, VMEM, VMEM],
        out_specs=VMEM,
        compiler_params=PARAMS,
    )(place, after(block_mask, own[0]), local[:, None], np.repeat(local, BLOCK)[None, :])

    near_pick = tuple((i, 0, i, 1, 2 * i) for i in range(half))
    far_pick = tuple((i, 0, i, 1, 2 * i + 1) for i in range(half))
    both_pick = tuple((2 * i, 0, 2 * i + 1, 0, i) for i in range(sources))
    outs = [None] * chunks
    waiting = []
    gate = None
    for j in range(1, chunks):
        got = spread(own[j] if gate is None else after(own[j], *gate))
        kv = got[:, 1:]
        far = across(kv if gate is None else after(kv, waiting[-1][1]), "zh", 1)
        near = gathered(kv, gather + ("c",))
        state = attend(bias, j, got[:, :1], near, near_pick, None, False)
        waiting.append((got, far, state))
        gate = (kv, far0)
    got = spread(after(jnp.concatenate([own[0], far0], axis=1), *waiting[-2][1:], kv))
    for j, (mine, far, state) in enumerate(waiting[:-1], 1):
        outs[j] = attend(bias, j, mine[:, :1], gathered(far, gather + ("c",)), far_pick, state, True)
    mine, far, state = waiting[-1]
    got = after(got, state, outs[-2])
    parts = [gathered(got[:, p : p + 1], gather + ("c",)) for p in range(1, 5)]
    all0 = [a for part in zip(*parts) for a in part]
    outs[0] = attend(bias, 0, after(got, far)[:, :1], all0, both_pick, None, True)
    ready = jnp.stack(outs[:-1], axis=1)
    early = spread(ready)
    far_all = gathered(far, gather + ("c",))
    outs[-1] = attend(bias, chunks - 1, mine[:, :1], far_all, far_pick, after(state, ready), True)
    late = spread(after(outs[-1], early))

    def project(part, j):
        flat = jnp.transpose(part, (1, 0, 2)).reshape(tok, width)
        rows = out_weight[j * width : (j + 1) * width]
        return jnp.dot(flat, rows, preferred_element_type=jnp.float32)

    early = after(early, outs[-1])
    total = sum(project(early[:, j], j) for j in range(chunks - 1))
    return (total + project(late, chunks - 1)).astype(jnp.bfloat16)


def solution(mesh):
    n_head, n_blk = mesh.shape["head"], mesh.shape["blk"]
    x, y = n_head // CORES, n_blk // PLANES
    shape = (x, CORES, 2, PLANES // 2, y)
    wide = Mesh(np.asarray(mesh.devices).reshape(shape), AXES)
    split, gather = (("x", "zl", "y"), ()) if x * y * 2 <= 8 else (("x", "zl"), ("y",))
    spec = P(AXES, None, None)
    return jax.shard_map(
        functools.partial(shards, split, gather),
        mesh=wide,
        in_specs=(spec, spec, spec, P(), P()),
        out_specs=P(AXES, None),
        check_vma=False,
    )
```

```python
import functools
import math

import jax
import jax.numpy as jnp
import numpy as np
from jax import lax
from jax.experimental import pallas as pl
from jax.experimental.pallas import tpu as pltpu
from jax.sharding import Mesh
from jax.sharding import PartitionSpec as P

BLOCK = 128
NEG = -1e30
CORES = 2
PLANES = 4
AXES = ("x", "c", "zh", "zl", "y")
VMEM = pl.BlockSpec(memory_space=pltpu.VMEM)
SMEM = pl.BlockSpec(memory_space=pltpu.SMEM)


def swap(size, bit):
    return [(i, i ^ bit) for i in range(size)]


def after(value, *others):
    return lax.optimization_barrier((value, *others))[0]


def grant(*arrays):
    held = sum(math.prod(a.shape) * a.dtype.itemsize for a in arrays)
    return pltpu.CompilerParams(vmem_limit_bytes=10 * 2**20 + 2 * held)


def bias_kernel(sources, chunk, place_ref, mask_ref, rows_ref, cols_ref, bias_ref):
    tiles, qb, _ = bias_ref.shape
    blocks = mask_ref.shape[1]
    span = cols_ref.shape[1]
    groups = tiles * qb
    group = place_ref[sources]
    lanes = lax.broadcasted_iota(jnp.int32, (groups, blocks), 1)
    mine = (lanes == rows_ref[...] + place_ref[0]).astype(jnp.bfloat16)
    mask = (mask_ref[chunk * groups + group] > 0).astype(jnp.bfloat16)
    rows = jnp.dot(mine, mask, preferred_element_type=jnp.float32).astype(jnp.bfloat16)
    depth = lax.broadcasted_iota(jnp.int32, (blocks, span), 0)
    for n in range(sources):
        pick = (depth == cols_ref[...] + place_ref[n]).astype(jnp.bfloat16)
        seen = jnp.dot(rows, pick, preferred_element_type=jnp.float32)
        bias = jnp.where(seen > 0.5, 0.0, NEG)
        bias_ref[:, :, n * span : (n + 1) * span] = bias.reshape(tiles, qb, span)


def attend_kernel(picks, count, sub, scale, first, last, *refs):
    bias_ref, q_ref = refs[:2]
    kv_refs = refs[2 : 2 + count]
    rest = refs[2 + count :]
    if not first:
        m_in, acc_in = rest[:2]
        rest = rest[2:]
    tiles, qb, _ = bias_ref.shape
    block, hdim = q_ref.shape[2:]
    rows = qb * block

    def tile(index, carry):
        q = q_ref[pl.ds(index * qb, qb), 0].reshape(rows, hdim)
        if first:
            m = jnp.full((rows, 1), NEG, jnp.float32)
            acc = jnp.zeros((rows, 2 * hdim), jnp.float32)
        else:
            m = jnp.max(m_in[pl.ds(index * rows, rows), :], axis=1, keepdims=True)
            acc = acc_in[pl.ds(index * rows, rows), :]
        for kref, kpart, vref, vpart, source in picks:
            span = kv_refs[kref].shape[0] * block
            for start in range(0, span, sub):
                some = slice(start // block, (start + sub) // block)
                k = kv_refs[kref][some, kpart].reshape(sub, hdim)
                v = kv_refs[vref][some, vpart].reshape(sub, hdim)
                v = jnp.concatenate([v, jnp.ones((sub, hdim), v.dtype)], axis=1)
                s = lax.dot_general(q, k, (((1,), (1,)), ((), ())), preferred_element_type=jnp.float32)
                at = source * span + start
                bias = bias_ref[index, :, at : at + sub]
                s = (s.reshape(qb, block, sub) * scale + bias[:, None, :]).reshape(rows, sub)
                m_next = jnp.maximum(m, jnp.max(s, axis=1, keepdims=True))
                p = jnp.exp2(s - m_next).astype(jnp.bfloat16)
                acc = acc * jnp.exp2(m - m_next) + jnp.dot(p, v, preferred_element_type=jnp.float32)
                m = m_next
        if last:
            out = (acc[:, :hdim] / acc[:, hdim:]).astype(jnp.bfloat16)
            rest[0][pl.ds(index * qb, qb)] = out.reshape(qb, block, hdim)
        else:
            rest[0][pl.ds(index * rows, rows), :] = jnp.broadcast_to(m, (rows, hdim))
            rest[1][pl.ds(index * rows, rows), :] = acc
        return carry

    lax.fori_loop(0, tiles, tile, 0)


def attend(bias, q, arrays, picks, state, last):
    groups, _, block, hdim = q.shape
    total = groups * block
    first = state is None
    if last:
        out_shape = jax.ShapeDtypeStruct((groups, block, hdim), jnp.bfloat16)
        out_specs = VMEM
    else:
        out_shape = (
            jax.ShapeDtypeStruct((total, hdim), jnp.float32),
            jax.ShapeDtypeStruct((total, 2 * hdim), jnp.float32),
        )
        out_specs = (VMEM, VMEM)
    args = [bias, q, *arrays, *(() if first else state)]
    scale = hdim**-0.5 * math.log2(math.e)
    keys = len(picks) * total
    sub = min(4, groups) * block
    return pl.pallas_call(
        functools.partial(attend_kernel, picks, len(arrays), sub, scale, first, last),
        out_shape=out_shape,
        in_specs=[VMEM] * len(args),
        out_specs=out_specs,
        compiler_params=grant(*args),
        cost_estimate=pl.CostEstimate(
            flops=total, bytes_accessed=4 * keys, transcendentals=0
        ),
    )(*args)


def shards(split, gather, queries, keys, values, block_mask, out_weight):
    sizes = {a: lax.axis_size(a) for a in AXES}
    stride = {a: math.prod(list(sizes.values())[i + 1 :]) for i, a in enumerate(AXES)}
    n_split = math.prod(sizes[a] for a in split)
    tok, heads, hdim = queries.shape
    chunks = heads // n_split
    width = n_split * hdim

    order = ("zh",) + gather + ("c",)
    bits = [dict(zip(reversed(order), b)) for b in np.ndindex(*(sizes[a] for a in reversed(order)))]
    sources = len(bits)
    half = sources // 2
    place = sum(
        (lax.axis_index(a) ^ np.array([b[a] for b in bits] + [0], np.int32)) * stride[a] for a in order
    )
    place = jnp.where(np.arange(sources + 1) == sources, lax.axis_index(split), place).astype(jnp.int32)
    local = np.zeros(1, np.int32)
    for a in split:
        local = (local[:, None] + np.arange(sizes[a], dtype=np.int32) * stride[a]).reshape(-1)
    qb = min(4, n_split)

    def across(a, axis, bit):
        return lax.ppermute(a, axis, swap(sizes[axis], bit))

    def spread(a):
        return lax.all_to_all(a, split, split_axis=0, concat_axis=0, tiled=True)

    def chunk(a, j):
        return jnp.transpose(a[:, j * n_split : (j + 1) * n_split], (1, 0, 2))

    def gathered(array, axes):
        arrays = [array]
        for a in axes:
            arrays = [p if bit == 0 else across(p, a, bit) for bit in range(sizes[a]) for p in arrays]
        return arrays

    first = jnp.stack([chunk(keys, 0), chunk(values, 0)], axis=1)
    far0 = across(first, "zh", 1)
    keys1, queries1, values1 = after((keys, queries, values), first)
    own = [jnp.stack([chunk(a, j) for a in (queries1, keys1, values1)], axis=1) for j in range(chunks)]
    own = [after(o, own[1]) if j != 1 else o for j, o in enumerate(own)]
    out = jax.ShapeDtypeStruct((n_split // qb, qb, sources * n_split * BLOCK), jnp.float32)

    def bias_of(j, *before):
        return pl.pallas_call(
            functools.partial(bias_kernel, sources, j),
            out_shape=out,
            in_specs=[SMEM, VMEM, VMEM, VMEM],
            out_specs=VMEM,
            compiler_params=grant(out, block_mask),
            cost_estimate=pl.CostEstimate(flops=10**11, bytes_accessed=0, transcendentals=0),
        )(place, after(block_mask, *before), local[:, None], np.repeat(local, BLOCK)[None, :])

    near_pick = tuple((i, 0, i, 1, 2 * i) for i in range(half))
    far_pick = tuple((i, 0, i, 1, 2 * i + 1) for i in range(half))
    both_pick = tuple((i, 1 + 2 * z, i, 2 + 2 * z, 2 * i + z) for i in range(half) for z in range(2))
    outs = [None] * chunks
    waiting = []
    far, gate = far0, ()
    for j in range(1, chunks):
        got = spread(after(own[j], *gate))
        bias = bias_of(j, far)
        got = after(got, bias)
        kv = got[:, 1:]
        gate = (kv,)
        far = across(kv, "zh", 1)
        near = gathered(kv, gather + ("c",))
        state = attend(bias, got[:, :1], near, near_pick, None, False)
        waiting.append((bias, got, far, state))
    got = spread(after(jnp.concatenate([own[0], far0], axis=1), kv))
    for j, (bias, mine, far, state) in enumerate(waiting[:-1], 1):
        outs[j] = attend(bias, mine[:, :1], gathered(far, gather + ("c",)), far_pick, state, True)
    bias, mine, far, state = waiting[-1]
    bias0 = bias_of(0, far)
    got = after(got, bias0, state, outs[-2])
    outs[0] = attend(bias0, got[:, :1], gathered(got, gather + ("c",)), both_pick, None, True)
    ready = jnp.stack(outs[:-1], axis=1)
    early = spread(ready)
    far_all = gathered(far, gather + ("c",))
    outs[-1] = attend(bias, mine[:, :1], far_all, far_pick, after(state, ready), True)
    late = spread(after(outs[-1], early))

    def project(part, j):
        flat = jnp.transpose(part, (1, 0, 2)).reshape(tok, width)
        rows = out_weight[j * width : (j + 1) * width]
        return jnp.dot(flat, rows, preferred_element_type=jnp.float32)

    early = after(early, outs[-1])
    total = sum(project(early[:, j], j) for j in range(chunks - 1))
    return (total + project(late, chunks - 1)).astype(jnp.bfloat16)


def solution(mesh):
    n_head, n_blk = mesh.shape["head"], mesh.shape["blk"]
    x, y = n_head // CORES, n_blk // PLANES
    shape = (x, CORES, 2, PLANES // 2, y)
    wide = Mesh(np.asarray(mesh.devices).reshape(shape), AXES)
    split, gather = (("x", "zl", "y"), ()) if x * y * 2 <= 8 else (("x", "zl"), ("y",))
    spec = P(AXES, None, None)
    return jax.shard_map(
        functools.partial(shards, split, gather),
        mesh=wide,
        in_specs=(spec, spec, spec, P(), P()),
        out_specs=P(AXES, None),
        check_vma=False,
    )
```

```python
import functools
import math

import jax
import jax.numpy as jnp
import numpy as np
from jax import lax
from jax.experimental import pallas as pl
from jax.experimental.pallas import tpu as pltpu
from jax.sharding import Mesh
from jax.sharding import PartitionSpec as P

BLOCK = 128
NEG = -1e30
CORES = 2
PLANES = 4
AXES = ("x", "c", "zh", "zl", "y")
VMEM = pl.BlockSpec(memory_space=pltpu.VMEM)
SMEM = pl.BlockSpec(memory_space=pltpu.SMEM)


def swap(size, bit):
    return [(i, i ^ bit) for i in range(size)]


def after(value, *others):
    return lax.optimization_barrier((value, *others))[0]


def grant(*arrays):
    held = sum(math.prod(a.shape) * a.dtype.itemsize for a in arrays)
    return pltpu.CompilerParams(vmem_limit_bytes=10 * 2**20 + 2 * held)


def bias_kernel(sources, chunk, place_ref, mask_ref, rows_ref, cols_ref, bias_ref):
    tiles, qb, _ = bias_ref.shape
    blocks = mask_ref.shape[1]
    span = cols_ref.shape[1]
    mask = (mask_ref[chunk * tiles * qb + place_ref[sources]] > 0).astype(jnp.bfloat16)
    lanes = lax.broadcasted_iota(jnp.int32, (qb, blocks), 1)
    depth = lax.broadcasted_iota(jnp.int32, (blocks, span), 0)
    rows = []
    for tile in range(tiles):
        mine = (lanes == rows_ref[...] + place_ref[tile]).astype(jnp.bfloat16)
        rows.append(jnp.dot(mine, mask, preferred_element_type=jnp.float32).astype(jnp.bfloat16))
    for n in range(sources):
        pick = (depth == cols_ref[...] + place_ref[n]).astype(jnp.bfloat16)
        for tile in range(tiles):
            seen = jnp.dot(rows[tile], pick, preferred_element_type=jnp.float32)
            bias_ref[tile, :, n * span : (n + 1) * span] = jnp.where(seen > 0.5, 0.0, NEG)


def attend_kernel(picks, count, scale, first, last, place_ref, bias_ref, q_ref, *refs):
    kv_refs, rest = refs[:count], refs[count:]
    if not first:
        m_in, acc_in = rest[:2]
        rest = rest[2:]
    tiles, qb, _ = bias_ref.shape
    block, hdim = q_ref.shape[2:]
    rows = qb * block

    def tile(index, carry):
        q = q_ref[:, 3 * index].reshape(rows, hdim)
        if first:
            m = jnp.full((rows, 1), NEG, jnp.float32)
            acc = jnp.zeros((rows, 2 * hdim), jnp.float32)
        else:
            m = jnp.max(m_in[pl.ds(index * rows, rows), :], axis=1, keepdims=True)
            acc = acc_in[pl.ds(index * rows, rows), :]
        for which, kpart, vpart, source in picks:
            k = kv_refs[which][:, kpart].reshape(rows, hdim)
            v = kv_refs[which][:, vpart].reshape(rows, hdim)
            v = jnp.concatenate([v, jnp.ones((rows, hdim), v.dtype)], axis=1)
            s = lax.dot_general(q, k, (((1,), (1,)), ((), ())), preferred_element_type=jnp.float32)
            bias = bias_ref[index, :, source * rows : (source + 1) * rows]
            s = (s.reshape(qb, block, rows) * scale + bias[:, None, :]).reshape(rows, rows)
            m_next = jnp.maximum(m, jnp.max(s, axis=1, keepdims=True))
            p = jnp.exp2(s - m_next).astype(jnp.bfloat16)
            acc = acc * jnp.exp2(m - m_next) + jnp.dot(p, v, preferred_element_type=jnp.float32)
            m = m_next
        if last:
            out = (acc[:, :hdim] / acc[:, hdim:]).astype(jnp.bfloat16)
            for row in range(qb):
                rest[0][place_ref[index * qb + row]] = out[row * block : (row + 1) * block]
        else:
            rest[0][pl.ds(index * rows, rows), :] = jnp.broadcast_to(m, (rows, hdim))
            rest[1][pl.ds(index * rows, rows), :] = acc
        return carry

    lax.fori_loop(0, tiles, tile, 0)


def attend(place, bias, q, arrays, picks, state, last):
    tiles, qb, _ = bias.shape
    block, hdim = q.shape[2:]
    groups = tiles * qb
    total = groups * block
    first = state is None
    if last:
        out_shape = jax.ShapeDtypeStruct((groups, block, hdim), jnp.bfloat16)
        out_specs = VMEM
    else:
        out_shape = (
            jax.ShapeDtypeStruct((total, hdim), jnp.float32),
            jax.ShapeDtypeStruct((total, 2 * hdim), jnp.float32),
        )
        out_specs = (VMEM, VMEM)
    args = [place, bias, q, *arrays, *(() if first else state)]
    scale = hdim**-0.5 * math.log2(math.e)
    return pl.pallas_call(
        functools.partial(attend_kernel, picks, len(arrays), scale, first, last),
        out_shape=out_shape,
        in_specs=[SMEM] + [VMEM] * (len(args) - 1),
        out_specs=out_specs,
        compiler_params=grant(*args),
        cost_estimate=pl.CostEstimate(flops=total, bytes_accessed=4 * total, transcendentals=0),
    )(*args)


def shards(split, gather, queries, keys, values, block_mask, out_weight):
    sizes = {a: lax.axis_size(a) for a in AXES}
    stride = {a: math.prod(list(sizes.values())[i + 1 :]) for i, a in enumerate(AXES)}
    flat = tuple(a for a in split if a != "zl")
    n_split = math.prod(sizes[a] for a in split)
    n_flat = math.prod(sizes[a] for a in flat)
    tok, heads, hdim = queries.shape
    chunks = heads // n_split
    width = n_split * hdim
    here = lax.axis_index("zl")

    order = ("zl", "zh") + gather + ("c",)
    bits = [dict(zip(reversed(order), b)) for b in np.ndindex(*(sizes[a] for a in reversed(order)))]
    sources = len(bits)
    half = sources // 4
    place = sum(
        (lax.axis_index(a) ^ np.array([b[a] for b in bits] + [0], np.int32)) * stride[a] for a in order
    )
    place = jnp.where(np.arange(sources + 1) == sources, lax.axis_index(split), place).astype(jnp.int32)
    local = np.zeros(1, np.int32)
    for a in flat:
        local = (local[:, None] + np.arange(sizes[a], dtype=np.int32) * stride[a]).reshape(-1)
    spot = np.arange(n_split).reshape([sizes[a] for a in split])
    spot = np.moveaxis(spot, split.index("zl"), 0).reshape(2, n_flat).astype(np.int32)
    home = jnp.where(here == 0, spot, spot[::-1]).reshape(-1)

    def across(a, axis, bit):
        n = math.prod(sizes[x] for x in axis) if isinstance(axis, tuple) else sizes[axis]
        return lax.ppermute(a, axis, swap(n, bit))

    def spread(a, axes):
        return lax.all_to_all(a, axes, split_axis=0, concat_axis=0, tiled=True)

    def pieces(arrays, j, bit):
        out = []
        for a in arrays:
            a = jnp.transpose(a[:, j * n_split : (j + 1) * n_split], (1, 0, 2))
            a = a.reshape([sizes[x] for x in split] + [tok, hdim])
            a = lax.dynamic_index_in_dim(a, here ^ bit, split.index("zl"), keepdims=False)
            out.append(a.reshape(n_flat, tok, hdim))
        return jnp.stack(out, axis=1)

    def gathered(array, axes):
        arrays = [array]
        for a in axes:
            arrays = [p if bit == 0 else across(p, a, bit) for bit in range(sizes[a]) for p in arrays]
        return arrays

    out = jax.ShapeDtypeStruct((2, n_flat, sources * n_flat * BLOCK), jnp.float32)

    def bias_of(j, *before):
        return pl.pallas_call(
            functools.partial(bias_kernel, sources, j),
            out_shape=out,
            in_specs=[SMEM, VMEM, VMEM, VMEM],
            out_specs=VMEM,
            compiler_params=grant(out, block_mask),
            cost_estimate=pl.CostEstimate(flops=3 * 10**9 if j else 8 * 10**9, bytes_accessed=0, transcendentals=0),
        )(place, after(block_mask, *before), local[:, None], np.repeat(local, BLOCK)[None, :])

    far0 = [across(pieces((keys, values), 0, b), ("zh", "zl"), 2 + b) for b in range(2)]
    trio = (queries, keys, values)
    own = []
    for j in (1, 2, 0) if chunks == 3 else range(chunks):
        own.append((j, pieces(trio, j, 0), across(pieces(trio, j, 1), "zl", 1)))
    own = {j: jnp.concatenate([mine, got], axis=1) for j, mine, got in own}

    near_pick = tuple((i, 2 * r, 2 * r + 1, 4 * i + r) for i in range(half) for r in range(2))
    far_pick = tuple((i, 2 * r, 2 * r + 1, 4 * i + 2 + r) for i in range(half) for r in range(2))
    both_pick = tuple((i, 1 + 3 * r, 2 + 3 * r, 4 * i + r) for i in range(half) for r in range(2))
    both_pick += tuple((i, 6 + 2 * r, 7 + 2 * r, 4 * i + 2 + r) for i in range(half) for r in range(2))
    axes = gather + ("c",)
    outs = [None] * chunks
    waiting = []
    far, gate = far0, ()
    for j in range(1, chunks):
        got = spread(after(own[j], *gate), flat)
        bias = bias_of(j, far)
        got = after(got, bias)
        kv = jnp.concatenate([got[:, 1:3], got[:, 4:6]], axis=1)
        gate = (kv,)
        far = across(kv, "zh", 1)
        near = gathered(kv, axes)
        state = attend(home, bias, got, near, near_pick, None, False)
        waiting.append((bias, got, far, state))
    got = spread(after(jnp.concatenate([own[0], *far0], axis=1), kv), flat)
    for j, (bias, mine, far, state) in enumerate(waiting[:-1], 1):
        outs[j] = attend(home, bias, mine, gathered(far, axes), far_pick, state, True)
    bias, mine, far, state = waiting[-1]
    bias0 = bias_of(0, far)
    got = after(got, bias0, state, outs[-2])
    outs[0] = attend(home, bias0, got, gathered(got, axes), both_pick, None, True)
    ready = jnp.stack(outs[:-1], axis=1)
    early = spread(ready, split)
    far_all = gathered(far, axes)
    outs[-1] = attend(home, bias, mine, far_all, far_pick, after(state, ready), True)
    late = spread(after(outs[-1], early), split)

    def project(part, j):
        joined = jnp.transpose(part, (1, 0, 2)).reshape(tok, width)
        rows = out_weight[j * width : (j + 1) * width]
        return jnp.dot(joined, rows, preferred_element_type=jnp.float32)

    early = after(early, outs[-1])
    total = sum(project(early[:, j], j) for j in range(chunks - 1))
    return (total + project(late, chunks - 1)).astype(jnp.bfloat16)


def solution(mesh):
    n_head, n_blk = mesh.shape["head"], mesh.shape["blk"]
    x, y = n_head // CORES, n_blk // PLANES
    shape = (x, CORES, 2, PLANES // 2, y)
    wide = Mesh(np.asarray(mesh.devices).reshape(shape), AXES)
    split, gather = (("x", "zl", "y"), ()) if x * y * 2 <= 8 else (("x", "zl"), ("y",))
    spec = P(AXES, None, None)
    return jax.shard_map(
        functools.partial(shards, split, gather),
        mesh=wide,
        in_specs=(spec, spec, spec, P(), P()),
        out_specs=P(AXES, None),
        check_vma=False,
    )
```

```python
import functools
import math

import jax
import jax.numpy as jnp
import numpy as np
from jax import lax
from jax.experimental import pallas as pl
from jax.experimental.pallas import tpu as pltpu
from jax.sharding import Mesh
from jax.sharding import PartitionSpec as P

BLOCK = 128
NEG = -1e30
CORES = 2
PLANES = 4
AXES = ("x", "c", "zh", "zl", "y")
VMEM = pl.BlockSpec(memory_space=pltpu.VMEM)
SMEM = pl.BlockSpec(memory_space=pltpu.SMEM)


def swap(size, bit):
    return [(i, i ^ bit) for i in range(size)]


def after(value, *others):
    return lax.optimization_barrier((value, *others))[0]


def grant(*arrays):
    held = sum(math.prod(a.shape) * a.dtype.itemsize for a in arrays)
    return pltpu.CompilerParams(vmem_limit_bytes=10 * 2**20 + 2 * held)


def bias_kernel(sources, chunk, place_ref, mask_ref, rows_ref, cols_ref, bias_ref):
    tiles, qb, _ = bias_ref.shape
    blocks = mask_ref.shape[1]
    span = cols_ref.shape[1]
    mask = (mask_ref[chunk * tiles * qb + place_ref[sources]] > 0).astype(jnp.bfloat16)
    lanes = lax.broadcasted_iota(jnp.int32, (qb, blocks), 1)
    depth = lax.broadcasted_iota(jnp.int32, (blocks, span), 0)
    rows = []
    for tile in range(tiles):
        mine = (lanes == rows_ref[...] + place_ref[tile]).astype(jnp.bfloat16)
        rows.append(jnp.dot(mine, mask, preferred_element_type=jnp.float32).astype(jnp.bfloat16))
    for n in range(sources):
        pick = (depth == cols_ref[...] + place_ref[n]).astype(jnp.bfloat16)
        for tile in range(tiles):
            seen = jnp.dot(rows[tile], pick, preferred_element_type=jnp.float32)
            bias_ref[tile, :, n * span : (n + 1) * span] = jnp.where(seen > 0.5, 0.0, NEG)


def attend_kernel(picks, count, qpart, scale, first, last, place_ref, bias_ref, q_ref, *refs):
    kv_refs, rest = refs[:count], refs[count:]
    if not first:
        m_in, acc_in = rest[:2]
        rest = rest[2:]
    tiles, qb, _ = bias_ref.shape
    block, hdim = q_ref.shape[2:]
    rows = qb * block

    def tile(index, carry):
        q = q_ref[:, qpart + 3 * index].reshape(rows, hdim)
        if first:
            m = jnp.full((rows, 1), NEG, jnp.float32)
            acc = jnp.zeros((rows, 2 * hdim), jnp.float32)
        else:
            m = jnp.max(m_in[pl.ds(index * rows, rows), :], axis=1, keepdims=True)
            acc = acc_in[pl.ds(index * rows, rows), :]
        for which, kpart, vpart, source in picks:
            k = kv_refs[which][:, kpart].reshape(rows, hdim)
            v = kv_refs[which][:, vpart].reshape(rows, hdim)
            v = jnp.concatenate([v, jnp.ones((rows, hdim), v.dtype)], axis=1)
            s = lax.dot_general(q, k, (((1,), (1,)), ((), ())), preferred_element_type=jnp.float32)
            bias = bias_ref[index, :, source * rows : (source + 1) * rows]
            s = (s.reshape(qb, block, rows) * scale + bias[:, None, :]).reshape(rows, rows)
            m_next = jnp.maximum(m, jnp.max(s, axis=1, keepdims=True))
            p = jnp.exp2(s - m_next).astype(jnp.bfloat16)
            acc = acc * jnp.exp2(m - m_next) + jnp.dot(p, v, preferred_element_type=jnp.float32)
            m = m_next
        if last:
            out = (acc[:, :hdim] / acc[:, hdim:]).astype(jnp.bfloat16)
            for row in range(qb):
                rest[0][place_ref[index * qb + row]] = out[row * block : (row + 1) * block]
        else:
            rest[0][pl.ds(index * rows, rows), :] = jnp.broadcast_to(m, (rows, hdim))
            rest[1][pl.ds(index * rows, rows), :] = acc
        return carry

    lax.fori_loop(0, tiles, tile, 0)


def attend(place, bias, q, qpart, arrays, picks, state, last):
    tiles, qb, _ = bias.shape
    block, hdim = q.shape[2:]
    groups = tiles * qb
    total = groups * block
    first = state is None
    if last:
        out_shape = jax.ShapeDtypeStruct((groups, block, hdim), jnp.bfloat16)
        out_specs = VMEM
    else:
        out_shape = (
            jax.ShapeDtypeStruct((total, hdim), jnp.float32),
            jax.ShapeDtypeStruct((total, 2 * hdim), jnp.float32),
        )
        out_specs = (VMEM, VMEM)
    args = [place, bias, q, *arrays, *(() if first else state)]
    scale = hdim**-0.5 * math.log2(math.e)
    return pl.pallas_call(
        functools.partial(attend_kernel, picks, len(arrays), qpart, scale, first, last),
        out_shape=out_shape,
        in_specs=[SMEM] + [VMEM] * (len(args) - 1),
        out_specs=out_specs,
        compiler_params=grant(*args),
        cost_estimate=pl.CostEstimate(flops=total, bytes_accessed=4 * total, transcendentals=0),
    )(*args)


def pack_kernel(takes, *refs):
    at = 0
    for ref, parts in zip(refs, takes):
        for part in parts:
            refs[-1][:, at] = ref[:, part]
            at += 1


def pack(*takes):
    arrays = [a for a, _ in takes]
    first = arrays[0]
    count = sum(len(parts) for _, parts in takes)
    return pl.pallas_call(
        functools.partial(pack_kernel, [tuple(parts) for _, parts in takes]),
        out_shape=jax.ShapeDtypeStruct((first.shape[0], count) + first.shape[2:], first.dtype),
        in_specs=[VMEM] * len(arrays),
        out_specs=VMEM,
        compiler_params=grant(*arrays),
        cost_estimate=pl.CostEstimate(flops=10**6, bytes_accessed=10**4, transcendentals=0),
    )(*arrays)


def finish_kernel(part_ref, rows_ref, total_ref, out_ref):
    pieces, tok, hdim = part_ref.shape
    joined = jnp.concatenate([part_ref[i] for i in range(pieces)], axis=1)
    step = math.gcd(out_ref.shape[1], 512)

    def columns(index, carry):
        at = pl.ds(pl.multiple_of(index * step, step), step)
        product = jnp.dot(joined, rows_ref[:, at], preferred_element_type=jnp.float32)
        out_ref[:, at] = (total_ref[:, at] + product).astype(out_ref.dtype)
        return carry

    lax.fori_loop(0, out_ref.shape[1] // step, columns, 0)


def finish(part, rows, total):
    return pl.pallas_call(
        finish_kernel,
        out_shape=jax.ShapeDtypeStruct(total.shape, jnp.bfloat16),
        in_specs=[VMEM] * 3,
        out_specs=VMEM,
        compiler_params=grant(part, rows, total),
    )(part, rows, total)


def shards(split, gather, queries, keys, values, block_mask, out_weight):
    sizes = {a: lax.axis_size(a) for a in AXES}
    stride = {a: math.prod(list(sizes.values())[i + 1 :]) for i, a in enumerate(AXES)}
    flat = tuple(a for a in split if a != "zl")
    n_split = math.prod(sizes[a] for a in split)
    n_flat = math.prod(sizes[a] for a in flat)
    tok, heads, hdim = queries.shape
    chunks = heads // n_split
    width = n_split * hdim
    here = lax.axis_index("zl")

    order = ("zl", "zh") + gather + ("c",)
    bits = [dict(zip(reversed(order), b)) for b in np.ndindex(*(sizes[a] for a in reversed(order)))]
    sources = len(bits)
    half = sources // 4
    place = sum(
        (lax.axis_index(a) ^ np.array([b[a] for b in bits] + [0], np.int32)) * stride[a] for a in order
    )
    place = jnp.where(np.arange(sources + 1) == sources, lax.axis_index(split), place).astype(jnp.int32)
    local = np.zeros(1, np.int32)
    for a in flat:
        local = (local[:, None] + np.arange(sizes[a], dtype=np.int32) * stride[a]).reshape(-1)
    spot = np.arange(n_split).reshape([sizes[a] for a in split])
    spot = np.moveaxis(spot, split.index("zl"), 0).reshape(2, n_flat).astype(np.int32)
    home = jnp.where(here == 0, spot, spot[::-1]).reshape(-1)

    def across(a, axis, bit):
        n = math.prod(sizes[x] for x in axis) if isinstance(axis, tuple) else sizes[axis]
        return lax.ppermute(a, axis, swap(n, bit))

    def spread(a, axes):
        return lax.all_to_all(a, axes, split_axis=0, concat_axis=0, tiled=True)

    def pieces(arrays, j, bit):
        out = []
        for a in arrays:
            a = jnp.transpose(a[:, j * n_split : (j + 1) * n_split], (1, 0, 2))
            a = a.reshape([sizes[x] for x in split] + [tok, hdim])
            a = lax.dynamic_index_in_dim(a, here ^ bit, split.index("zl"), keepdims=False)
            out.append(a.reshape(n_flat, tok, hdim))
        return jnp.stack(out, axis=1)

    def gathered(array, axes):
        arrays = [array]
        for a in axes:
            arrays = [p if bit == 0 else across(p, a, bit) for bit in range(sizes[a]) for p in arrays]
        return arrays

    out = jax.ShapeDtypeStruct((2, n_flat, sources * n_flat * BLOCK), jnp.float32)

    def bias_of(j, *before):
        return pl.pallas_call(
            functools.partial(bias_kernel, sources, j),
            out_shape=out,
            in_specs=[SMEM, VMEM, VMEM, VMEM],
            out_specs=VMEM,
            compiler_params=grant(out, block_mask),
            cost_estimate=pl.CostEstimate(flops={1: 3 * 10**9, 2: 2 * 10**10}.get(j, 10**6), bytes_accessed=0, transcendentals=0),
        )(place, after(block_mask, *before), local[:, None], np.repeat(local, BLOCK)[None, :])

    far0 = [across(pieces((keys, values), 0, b), ("zh", "zl"), 2 + b) for b in range(2)]
    trio = (queries, keys, values)
    own = []
    for j in (1, 2, 0):
        own.append((j, pieces(trio, j, 0), across(pieces(trio, j, 1), "zl", 1)))
    own = {j: ((mine, range(3)), (got, range(3))) for j, mine, got in own}
    assert chunks == 3

    near_pick = tuple((i, 2 * r, 2 * r + 1, 4 * i + r) for i in range(half) for r in range(2))
    far_pick = tuple((i, 2 * r, 2 * r + 1, 4 * i + 2 + r) for i in range(half) for r in range(2))
    mine_pick = tuple((i, 1 + 3 * r, 2 + 3 * r, 4 * i + r) for i in range(half) for r in range(2))
    both_pick = tuple((i, 7 + 3 * r, 8 + 3 * r, 4 * i + r) for i in range(half) for r in range(2))
    both_pick += tuple((i, 12 + 2 * r, 13 + 2 * r, 4 * i + 2 + r) for i in range(half) for r in range(2))
    axes = gather + ("c",)

    def keyed(got):
        return pack((got, (1, 2, 4, 5)))

    got1 = spread(pack(*own[1]), flat)
    bias1 = bias_of(1, *far0)
    both = pack(*own[2], *own[0], *((f, range(2)) for f in far0))
    got1 = after(got1, bias1, both)
    kv1 = keyed(got1)
    far1 = across(kv1, "zh", 1)
    state1 = attend(home, bias1, got1, 0, gathered(kv1, axes), near_pick, None, False)
    got = spread(after(both, kv1), flat)
    bias2 = bias_of(2, far1)
    got = after(got, bias2, state1)
    kv2 = keyed(got)
    far2 = across(kv2, "zh", 1)
    shared = gathered(after(got, kv2), axes)
    out1 = attend(home, bias1, got1, 0, gathered(far1, axes), far_pick, state1, True)
    state2 = attend(home, bias2, got, 0, shared, mine_pick, None, False)
    bias0 = bias_of(0, bias2)
    out0 = attend(home, bias0, after(got, out1, state2[0]), 6, shared, both_pick, None, True)
    ready = jnp.stack([out0, out1], axis=1)
    early = spread(ready, split)
    out2 = attend(home, bias2, got, 0, gathered(far2, axes), far_pick, after(state2, ready), True)
    late = spread(after(out2, early), split)

    rows = 2 * width
    early = jnp.transpose(after(early, out2), (2, 1, 0, 3)).reshape(tok, rows)
    total = jnp.dot(early, out_weight[:rows], preferred_element_type=jnp.float32)
    return finish(late, out_weight[rows:], total)


def solution(mesh):
    n_head, n_blk = mesh.shape["head"], mesh.shape["blk"]
    x, y = n_head // CORES, n_blk // PLANES
    shape = (x, CORES, 2, PLANES // 2, y)
    wide = Mesh(np.asarray(mesh.devices).reshape(shape), AXES)
    split, gather = (("x", "zl", "y"), ()) if x * y * 2 <= 8 else (("x", "zl"), ("y",))
    spec = P(AXES, None, None)
    return jax.shard_map(
        functools.partial(shards, split, gather),
        mesh=wide,
        in_specs=(spec, spec, spec, P(), P()),
        out_specs=P(AXES, None),
        check_vma=False,
    )
```

```python
import functools
import math

import jax
import jax.numpy as jnp
import numpy as np
from jax import lax
from jax.experimental import pallas as pl
from jax.experimental.pallas import tpu as pltpu
from jax.sharding import Mesh
from jax.sharding import PartitionSpec as P

BLOCK = 128
NEG = -1e30
CORES = 2
PLANES = 4
AXES = ("x", "c", "zh", "zl", "y")
VMEM = pl.BlockSpec(memory_space=pltpu.VMEM)
SMEM = pl.BlockSpec(memory_space=pltpu.SMEM)


def swap(size, bit):
    return [(i, i ^ bit) for i in range(size)]


def after(value, *others):
    return lax.optimization_barrier((value, *others))[0]


def grant(*arrays):
    held = sum(math.prod(a.shape) * a.dtype.itemsize for a in arrays)
    return pltpu.CompilerParams(vmem_limit_bytes=10 * 2**20 + 2 * held)


def bias_kernel(sources, chunk, place_ref, mask_ref, rows_ref, cols_ref, bias_ref):
    tiles, qb, _ = bias_ref.shape
    blocks = mask_ref.shape[1]
    span = cols_ref.shape[1]
    mask = (mask_ref[chunk * tiles * qb + place_ref[sources]] > 0).astype(jnp.bfloat16)
    lanes = lax.broadcasted_iota(jnp.int32, (qb, blocks), 1)
    depth = lax.broadcasted_iota(jnp.int32, (blocks, span), 0)
    rows = []
    for tile in range(tiles):
        mine = (lanes == rows_ref[...] + place_ref[tile]).astype(jnp.bfloat16)
        rows.append(jnp.dot(mine, mask, preferred_element_type=jnp.float32).astype(jnp.bfloat16))
    for n in range(sources):
        pick = (depth == cols_ref[...] + place_ref[n]).astype(jnp.bfloat16)
        for tile in range(tiles):
            seen = jnp.dot(rows[tile], pick, preferred_element_type=jnp.float32)
            bias_ref[tile, :, n * span : (n + 1) * span] = jnp.where(seen > 0.5, 0.0, NEG)


def attend_kernel(picks, count, scale, first, last, place_ref, bias_ref, q_ref, *refs):
    kv_refs, rest = refs[:count], refs[count:]
    if not first:
        m_in, acc_in = rest[:2]
        rest = rest[2:]
    tiles, qb, _ = bias_ref.shape
    block, hdim = q_ref.shape[2:]
    rows = qb * block

    def tile(index, carry):
        q = q_ref[:, 3 * index].reshape(rows, hdim)
        if first:
            m = jnp.full((rows, 1), NEG, jnp.float32)
            acc = jnp.zeros((rows, 2 * hdim), jnp.float32)
        else:
            m = jnp.max(m_in[pl.ds(index * rows, rows), :], axis=1, keepdims=True)
            acc = acc_in[pl.ds(index * rows, rows), :]
        for which, kpart, vpart, source in picks:
            k = kv_refs[which][:, kpart].reshape(rows, hdim)
            v = kv_refs[which][:, vpart].reshape(rows, hdim)
            v = jnp.concatenate([v, jnp.ones((rows, hdim), v.dtype)], axis=1)
            s = lax.dot_general(q, k, (((1,), (1,)), ((), ())), preferred_element_type=jnp.float32)
            bias = bias_ref[index, :, source * rows : (source + 1) * rows]
            s = (s.reshape(qb, block, rows) * scale + bias[:, None, :]).reshape(rows, rows)
            m_next = jnp.maximum(m, jnp.max(s, axis=1, keepdims=True))
            p = jnp.exp2(s - m_next).astype(jnp.bfloat16)
            acc = acc * jnp.exp2(m - m_next) + jnp.dot(p, v, preferred_element_type=jnp.float32)
            m = m_next
        if last:
            out = (acc[:, :hdim] / acc[:, hdim:]).astype(jnp.bfloat16)
            for row in range(qb):
                rest[0][place_ref[index * qb + row]] = out[row * block : (row + 1) * block]
        else:
            rest[0][pl.ds(index * rows, rows), :] = jnp.broadcast_to(m, (rows, hdim))
            rest[1][pl.ds(index * rows, rows), :] = acc
        return carry

    lax.fori_loop(0, tiles, tile, 0)


def attend(place, bias, q, arrays, picks, state, last):
    tiles, qb, _ = bias.shape
    block, hdim = q.shape[2:]
    groups = tiles * qb
    total = groups * block
    first = state is None
    if last:
        out_shape = jax.ShapeDtypeStruct((groups, block, hdim), jnp.bfloat16)
        out_specs = VMEM
    else:
        out_shape = (
            jax.ShapeDtypeStruct((total, hdim), jnp.float32),
            jax.ShapeDtypeStruct((total, 2 * hdim), jnp.float32),
        )
        out_specs = (VMEM, VMEM)
    args = [place, bias, q, *arrays, *(() if first else state)]
    scale = hdim**-0.5 * math.log2(math.e)
    return pl.pallas_call(
        functools.partial(attend_kernel, picks, len(arrays), scale, first, last),
        out_shape=out_shape,
        in_specs=[SMEM] + [VMEM] * (len(args) - 1),
        out_specs=out_specs,
        compiler_params=grant(*args),
        cost_estimate=pl.CostEstimate(flops=total, bytes_accessed=4 * total, transcendentals=0),
    )(*args)


def pack_kernel(takes, *refs):
    at = 0
    for ref, parts in zip(refs, takes):
        for part in parts:
            refs[-1][:, at] = ref[:, part]
            at += 1


def pack(*takes):
    arrays = [a for a, _ in takes]
    first = arrays[0]
    count = sum(len(parts) for _, parts in takes)
    return pl.pallas_call(
        functools.partial(pack_kernel, [tuple(parts) for _, parts in takes]),
        out_shape=jax.ShapeDtypeStruct((first.shape[0], count) + first.shape[2:], first.dtype),
        in_specs=[VMEM] * len(arrays),
        out_specs=VMEM,
        compiler_params=grant(*arrays),
        cost_estimate=pl.CostEstimate(flops=10**6, bytes_accessed=10**4, transcendentals=0),
    )(*arrays)


def finish_kernel(part_ref, rows_ref, total_ref, out_ref):
    joined = jnp.concatenate([part_ref[i] for i in range(part_ref.shape[0])], axis=1)
    product = jnp.dot(joined, rows_ref[...], preferred_element_type=jnp.float32)
    out_ref[...] = (total_ref[...] + product).astype(out_ref.dtype)


def finish(part, weight, total):
    pieces, tok, hdim = part.shape
    width = pieces * hdim
    last = weight.shape[0] // width - 1
    step = math.gcd(weight.shape[1], 768)
    return pl.pallas_call(
        finish_kernel,
        out_shape=jax.ShapeDtypeStruct(total.shape, jnp.bfloat16),
        grid=(weight.shape[1] // step,),
        in_specs=[
            pl.BlockSpec((pieces, tok, hdim), lambda i: (0, 0, 0)),
            pl.BlockSpec((width, step), lambda i: (last, i)),
            pl.BlockSpec((tok, step), lambda i: (0, i)),
        ],
        out_specs=pl.BlockSpec((tok, step), lambda i: (0, i)),
        compiler_params=grant(part, total),
    )(part, weight, total)


def shards(split, gather, queries, keys, values, block_mask, out_weight):
    sizes = {a: lax.axis_size(a) for a in AXES}
    stride = {a: math.prod(list(sizes.values())[i + 1 :]) for i, a in enumerate(AXES)}
    flat = tuple(a for a in split if a != "zl")
    n_split = math.prod(sizes[a] for a in split)
    n_flat = math.prod(sizes[a] for a in flat)
    tok, heads, hdim = queries.shape
    chunks = heads // n_split
    width = n_split * hdim
    here = lax.axis_index("zl")

    order = ("zl", "zh") + gather + ("c",)
    bits = [dict(zip(reversed(order), b)) for b in np.ndindex(*(sizes[a] for a in reversed(order)))]
    sources = len(bits)
    half = sources // 4
    place = sum(
        (lax.axis_index(a) ^ np.array([b[a] for b in bits] + [0], np.int32)) * stride[a] for a in order
    )
    place = jnp.where(np.arange(sources + 1) == sources, lax.axis_index(split), place).astype(jnp.int32)
    local = np.zeros(1, np.int32)
    for a in flat:
        local = (local[:, None] + np.arange(sizes[a], dtype=np.int32) * stride[a]).reshape(-1)
    spot = np.arange(n_split).reshape([sizes[a] for a in split])
    spot = np.moveaxis(spot, split.index("zl"), 0).reshape(2, n_flat).astype(np.int32)
    home = jnp.where(here == 0, spot, spot[::-1]).reshape(-1)

    def across(a, axis, bit):
        n = math.prod(sizes[x] for x in axis) if isinstance(axis, tuple) else sizes[axis]
        return lax.ppermute(a, axis, swap(n, bit))

    def spread(a, axes):
        return lax.all_to_all(a, axes, split_axis=0, concat_axis=0, tiled=True)

    def pieces(arrays, j, bit):
        out = []
        for a in arrays:
            a = jnp.transpose(a[:, j * n_split : (j + 1) * n_split], (1, 0, 2))
            a = a.reshape([sizes[x] for x in split] + [tok, hdim])
            a = lax.dynamic_index_in_dim(a, here ^ bit, split.index("zl"), keepdims=False)
            out.append(a.reshape(n_flat, tok, hdim))
        return jnp.stack(out, axis=1)

    def gathered(array, axes):
        arrays = [array]
        for a in axes:
            arrays = [p if bit == 0 else across(p, a, bit) for bit in range(sizes[a]) for p in arrays]
        return arrays

    out = jax.ShapeDtypeStruct((2, n_flat, sources * n_flat * BLOCK), jnp.float32)

    def bias_of(j, *before):
        return pl.pallas_call(
            functools.partial(bias_kernel, sources, j),
            out_shape=out,
            in_specs=[SMEM, VMEM, VMEM, VMEM],
            out_specs=VMEM,
            compiler_params=grant(out, block_mask),
            cost_estimate=pl.CostEstimate(flops={2: 3 * 10**9, 0: 8 * 10**9, 1: 8 * 10**9}[j], bytes_accessed=0, transcendentals=0),
        )(place, after(block_mask, *before), local[:, None], np.repeat(local, BLOCK)[None, :])

    assert chunks == 3
    trio = (queries, keys, values)

    def cross(j, *before):
        halves = [pieces((keys, values), j, b) for b in range(2)]
        if before:
            halves = after(halves, *before)
        return [across(h, ("zh", "zl"), 2 + b) for b, h in enumerate(halves)]

    def own(j, *before):
        given = pieces(trio, j, 1)
        if before:
            given = after(given, *before)
        return (pieces(trio, j, 0), range(3)), (across(given, "zl", 1), range(3))

    near_pick = tuple((i, 2 * r, 2 * r + 1, 4 * i + r) for i in range(half) for r in range(2))
    far_pick = tuple((i, 2 * r, 2 * r + 1, 4 * i + 2 + r) for i in range(half) for r in range(2))
    both_pick = tuple((i, 1 + 3 * r, 2 + 3 * r, 4 * i + r) for i in range(half) for r in range(2))
    both_pick += tuple((i, 6 + 2 * r, 7 + 2 * r, 4 * i + 2 + r) for i in range(half) for r in range(2))
    axes = gather + ("c",)

    far0 = cross(0)
    own2 = own(2)
    got2 = spread(pack(*own2), flat)
    bias2 = bias_of(2, *far0)
    own0 = pack(*own(0, own2[1][0]), *((f, range(2)) for f in far0))
    got2 = after(got2, bias2, own0)
    kv2 = pack((got2, (1, 2, 4, 5)))
    far1 = cross(1, *far0)
    got0 = spread(after(own0, kv2), flat)
    bias0 = bias_of(0, *far1)
    state2 = attend(home, bias2, got2, gathered(kv2, axes), near_pick, None, False)
    own1 = pack(*own(1, *far0), *((f, range(2)) for f in far1))
    got0 = after(got0, bias0, own1, state2)
    far2 = across(after(kv2, *far1), "zh", 1)
    got1 = spread(after(own1, got0), flat)
    bias1 = bias_of(1, far2)
    out0 = attend(home, bias0, got0, gathered(got0, axes), both_pick, None, True)
    got1 = after(got1, bias1, out0)
    far2 = gathered(far2, axes)
    out1 = attend(home, bias1, got1, gathered(got1, axes), both_pick, None, True)
    ready = jnp.stack([out0, out1], axis=1)
    early = spread(ready, split)
    out2 = attend(home, bias2, got2, far2, far_pick, after(state2, ready), True)
    late = spread(after(out2, early), split)

    rows = 2 * width
    early = jnp.transpose(after(early, out2), (2, 1, 0, 3)).reshape(tok, rows)
    total = jnp.dot(early, out_weight[:rows], preferred_element_type=jnp.float32)
    return finish(late, out_weight, total)


def solution(mesh):
    n_head, n_blk = mesh.shape["head"], mesh.shape["blk"]
    x, y = n_head // CORES, n_blk // PLANES
    shape = (x, CORES, 2, PLANES // 2, y)
    wide = Mesh(np.asarray(mesh.devices).reshape(shape), AXES)
    split, gather = (("x", "zl", "y"), ()) if x * y * 2 <= 8 else (("x", "zl"), ("y",))
    spec = P(AXES, None, None)
    return jax.shard_map(
        functools.partial(shards, split, gather),
        mesh=wide,
        in_specs=(spec, spec, spec, P(), P()),
        out_specs=P(AXES, None),
        check_vma=False,
    )
```

```python
import functools
import math

import jax
import jax.numpy as jnp
import numpy as np
from jax import lax
from jax.experimental import pallas as pl
from jax.experimental.pallas import tpu as pltpu
from jax.sharding import Mesh
from jax.sharding import PartitionSpec as P

BLOCK = 128
NEG = -1e30
CORES = 2
PLANES = 4
AXES = ("x", "c", "zh", "zl", "y")
VMEM = pl.BlockSpec(memory_space=pltpu.VMEM)
SMEM = pl.BlockSpec(memory_space=pltpu.SMEM)


def swap(size, bit):
    return [(i, i ^ bit) for i in range(size)]


def after(value, *others):
    return lax.optimization_barrier((value, *others))[0]


def grant(*arrays):
    held = sum(math.prod(a.shape) * a.dtype.itemsize for a in arrays)
    return pltpu.CompilerParams(vmem_limit_bytes=10 * 2**20 + 2 * held)


def bias_kernel(sources, chunk, place_ref, mask_ref, rows_ref, cols_ref, bias_ref):
    tiles, qb, _ = bias_ref.shape
    blocks = mask_ref.shape[1]
    span = cols_ref.shape[1]
    mask = (mask_ref[chunk * tiles * qb + place_ref[sources]] > 0).astype(jnp.bfloat16)
    lanes = lax.broadcasted_iota(jnp.int32, (qb, blocks), 1)
    depth = lax.broadcasted_iota(jnp.int32, (blocks, span), 0)
    rows = []
    for tile in range(tiles):
        mine = (lanes == rows_ref[...] + place_ref[tile]).astype(jnp.bfloat16)
        rows.append(jnp.dot(mine, mask, preferred_element_type=jnp.float32).astype(jnp.bfloat16))
    for n in range(sources):
        pick = (depth == cols_ref[...] + place_ref[n]).astype(jnp.bfloat16)
        for tile in range(tiles):
            seen = jnp.dot(rows[tile], pick, preferred_element_type=jnp.float32)
            bias_ref[tile, :, n * span : (n + 1) * span] = jnp.where(seen > 0.5, 0.0, NEG)


def attend_kernel(picks, count, scale, first, last, place_ref, bias_ref, q_ref, *refs):
    kv_refs, rest = refs[:count], refs[count:]
    if not first:
        m_in, acc_in = rest[:2]
        rest = rest[2:]
    tiles, qb, _ = bias_ref.shape
    block, hdim = q_ref.shape[2:]
    rows = qb * block

    def tile(index, carry):
        q = q_ref[:, 3 * index].reshape(rows, hdim)
        if first:
            m = jnp.full((rows, 1), NEG, jnp.float32)
            acc = jnp.zeros((rows, 2 * hdim), jnp.float32)
        else:
            m = jnp.max(m_in[pl.ds(index * rows, rows), :], axis=1, keepdims=True)
            acc = acc_in[pl.ds(index * rows, rows), :]
        for which, kpart, vpart, source in picks:
            k = kv_refs[which][:, kpart].reshape(rows, hdim)
            v = kv_refs[which][:, vpart].reshape(rows, hdim)
            v = jnp.concatenate([v, jnp.ones((rows, hdim), v.dtype)], axis=1)
            s = lax.dot_general(q, k, (((1,), (1,)), ((), ())), preferred_element_type=jnp.float32)
            bias = bias_ref[index, :, source * rows : (source + 1) * rows]
            s = (s.reshape(qb, block, rows) * scale + bias[:, None, :]).reshape(rows, rows)
            m_next = jnp.maximum(m, jnp.max(s, axis=1, keepdims=True))
            p = jnp.exp2(s - m_next).astype(jnp.bfloat16)
            acc = acc * jnp.exp2(m - m_next) + jnp.dot(p, v, preferred_element_type=jnp.float32)
            m = m_next
        if last:
            out = (acc[:, :hdim] / acc[:, hdim:]).astype(jnp.bfloat16)
            for row in range(qb):
                rest[0][place_ref[index * qb + row]] = out[row * block : (row + 1) * block]
        else:
            rest[0][pl.ds(index * rows, rows), :] = jnp.broadcast_to(m, (rows, hdim))
            rest[1][pl.ds(index * rows, rows), :] = acc
        return carry

    lax.fori_loop(0, tiles, tile, 0)


def attend(place, bias, q, arrays, picks, state, last):
    tiles, qb, _ = bias.shape
    block, hdim = q.shape[2:]
    groups = tiles * qb
    total = groups * block
    first = state is None
    if last:
        out_shape = jax.ShapeDtypeStruct((groups, block, hdim), jnp.bfloat16)
        out_specs = VMEM
    else:
        out_shape = (
            jax.ShapeDtypeStruct((total, hdim), jnp.float32),
            jax.ShapeDtypeStruct((total, 2 * hdim), jnp.float32),
        )
        out_specs = (VMEM, VMEM)
    args = [place, bias, q, *arrays, *(() if first else state)]
    scale = hdim**-0.5 * math.log2(math.e)
    return pl.pallas_call(
        functools.partial(attend_kernel, picks, len(arrays), scale, first, last),
        out_shape=out_shape,
        in_specs=[SMEM] + [VMEM] * (len(args) - 1),
        out_specs=out_specs,
        compiler_params=grant(*args),
        cost_estimate=pl.CostEstimate(flops=total, bytes_accessed=4 * total, transcendentals=0),
    )(*args)


def pack_kernel(takes, *refs):
    at = 0
    for ref, parts in zip(refs, takes):
        for part in parts:
            refs[-1][:, at] = ref[:, part]
            at += 1


def pack(*takes):
    arrays = [a for a, _ in takes]
    first = arrays[0]
    count = sum(len(parts) for _, parts in takes)
    return pl.pallas_call(
        functools.partial(pack_kernel, [tuple(parts) for _, parts in takes]),
        out_shape=jax.ShapeDtypeStruct((first.shape[0], count) + first.shape[2:], first.dtype),
        in_specs=[VMEM] * len(arrays),
        out_specs=VMEM,
        compiler_params=grant(*arrays),
        cost_estimate=pl.CostEstimate(flops=10**6, bytes_accessed=10**4, transcendentals=0),
    )(*arrays)


def finish_kernel(step, part_ref, weight_ref, total_ref, out_ref, rows_ref, sems):
    width = rows_ref.shape[1]
    first = weight_ref.shape[0] - width
    copies = []
    for i in range(rows_ref.shape[0]):
        source = weight_ref.at[first:, i * step : (i + 1) * step]
        copies.append(pltpu.make_async_copy(source, rows_ref.at[i], sems.at[i]))
        copies[i].start()
    joined = jnp.concatenate([part_ref[i] for i in range(part_ref.shape[0])], axis=1)
    for i, copy in enumerate(copies):
        copy.wait()
        at = slice(i * step, (i + 1) * step)
        product = jnp.dot(joined, rows_ref[i], preferred_element_type=jnp.float32)
        out_ref[:, at] = (total_ref[:, at] + product).astype(out_ref.dtype)


def finish(part, weight, total):
    pieces, _, hdim = part.shape
    step = math.gcd(weight.shape[1], 512)
    count = weight.shape[1] // step
    rows = jax.ShapeDtypeStruct((count, pieces * hdim, step), weight.dtype)
    return pl.pallas_call(
        functools.partial(finish_kernel, step),
        out_shape=jax.ShapeDtypeStruct(total.shape, jnp.bfloat16),
        in_specs=[VMEM, pl.BlockSpec(memory_space=pl.ANY), VMEM],
        out_specs=VMEM,
        scratch_shapes=[pltpu.VMEM(rows.shape, rows.dtype), pltpu.SemaphoreType.DMA((count,))],
        compiler_params=grant(part, rows, total),
    )(part, weight, total)


def shards(split, gather, queries, keys, values, block_mask, out_weight):
    sizes = {a: lax.axis_size(a) for a in AXES}
    stride = {a: math.prod(list(sizes.values())[i + 1 :]) for i, a in enumerate(AXES)}
    flat = tuple(a for a in split if a != "zl")
    n_split = math.prod(sizes[a] for a in split)
    n_flat = math.prod(sizes[a] for a in flat)
    tok, heads, hdim = queries.shape
    chunks = heads // n_split
    width = n_split * hdim
    here = lax.axis_index("zl")

    order = ("zl", "zh") + gather + ("c",)
    bits = [dict(zip(reversed(order), b)) for b in np.ndindex(*(sizes[a] for a in reversed(order)))]
    sources = len(bits)
    half = sources // 4
    place = sum(
        (lax.axis_index(a) ^ np.array([b[a] for b in bits] + [0], np.int32)) * stride[a] for a in order
    )
    place = jnp.where(np.arange(sources + 1) == sources, lax.axis_index(split), place).astype(jnp.int32)
    local = np.zeros(1, np.int32)
    for a in flat:
        local = (local[:, None] + np.arange(sizes[a], dtype=np.int32) * stride[a]).reshape(-1)
    spot = np.arange(n_split).reshape([sizes[a] for a in split])
    spot = np.moveaxis(spot, split.index("zl"), 0).reshape(2, n_flat).astype(np.int32)
    home = jnp.where(here == 0, spot, spot[::-1]).reshape(-1)

    def across(a, axis, bit):
        n = math.prod(sizes[x] for x in axis) if isinstance(axis, tuple) else sizes[axis]
        return lax.ppermute(a, axis, swap(n, bit))

    def spread(a, axes):
        return lax.all_to_all(a, axes, split_axis=0, concat_axis=0, tiled=True)

    def pieces(arrays, j, bit):
        out = []
        for a in arrays:
            a = jnp.transpose(a[:, j * n_split : (j + 1) * n_split], (1, 0, 2))
            a = a.reshape([sizes[x] for x in split] + [tok, hdim])
            a = lax.dynamic_index_in_dim(a, here ^ bit, split.index("zl"), keepdims=False)
            out.append(a.reshape(n_flat, tok, hdim))
        return jnp.stack(out, axis=1)

    def gathered(array, axes):
        arrays = [array]
        for a in axes:
            arrays = [p if bit == 0 else across(p, a, bit) for bit in range(sizes[a]) for p in arrays]
        return arrays

    out = jax.ShapeDtypeStruct((2, n_flat, sources * n_flat * BLOCK), jnp.float32)

    def bias_of(j, *before):
        return pl.pallas_call(
            functools.partial(bias_kernel, sources, j),
            out_shape=out,
            in_specs=[SMEM, VMEM, VMEM, VMEM],
            out_specs=VMEM,
            compiler_params=grant(out, block_mask),
            cost_estimate=pl.CostEstimate(flops={2: 3 * 10**9, 0: 8 * 10**9, 1: 8 * 10**9}[j], bytes_accessed=0, transcendentals=0),
        )(place, after(block_mask, *before), local[:, None], np.repeat(local, BLOCK)[None, :])

    assert chunks == 3
    trio = (queries, keys, values)

    def cross(j, *before):
        halves = [pieces((keys, values), j, b) for b in range(2)]
        if before:
            halves = after(halves, *before)
        return [across(h, ("zh", "zl"), 2 + b) for b, h in enumerate(halves)]

    def own(j, *before):
        given = pieces(trio, j, 1)
        if before:
            given = after(given, *before)
        return (pieces(trio, j, 0), range(3)), (across(given, "zl", 1), range(3))

    near_pick = tuple((i, 2 * r, 2 * r + 1, 4 * i + r) for i in range(half) for r in range(2))
    far_pick = tuple((i, 2 * r, 2 * r + 1, 4 * i + 2 + r) for i in range(half) for r in range(2))
    both_pick = tuple((i, 1 + 3 * r, 2 + 3 * r, 4 * i + r) for i in range(half) for r in range(2))
    both_pick += tuple((i, 6 + 2 * r, 7 + 2 * r, 4 * i + 2 + r) for i in range(half) for r in range(2))
    axes = gather + ("c",)

    own2 = own(2)
    far0 = cross(0, own2[0][0])
    got2 = spread(pack(*own2), flat)
    bias2 = bias_of(2, *far0)
    own0 = pack(*own(0, own2[1][0]), *((f, range(2)) for f in far0))
    got2 = after(got2, bias2, own0)
    kv2 = pack((got2, (1, 2, 4, 5)))
    far1 = cross(1, own2[1][0])
    got0 = spread(after(own0, kv2), flat)
    bias0 = bias_of(0, *far1)
    state2 = attend(home, bias2, got2, gathered(kv2, axes), near_pick, None, False)
    own1 = pack(*own(1, *far0), *((f, range(2)) for f in far1))
    got0 = after(got0, bias0, own1, state2)
    far2 = across(kv2, "zh", 1)
    got1 = spread(after(own1, got0), flat)
    out0 = attend(home, bias0, got0, gathered(got0, axes), both_pick, None, True)
    bias1 = bias_of(1, far2, out0)
    got1 = after(got1, bias1)
    far2 = gathered(far2, axes)
    out1 = attend(home, bias1, got1, gathered(got1, axes), both_pick, None, True)
    ready = jnp.stack([out0, out1], axis=1)
    early = spread(ready, split)
    out2 = attend(home, bias2, got2, far2, far_pick, after(state2, ready), True)
    late = spread(after(out2, early), split)

    rows = 2 * width
    early = jnp.transpose(after(early, out2), (2, 1, 0, 3)).reshape(tok, rows)
    total = jnp.dot(early, out_weight[:rows], preferred_element_type=jnp.float32)
    return finish(late, out_weight, total)


def solution(mesh):
    n_head, n_blk = mesh.shape["head"], mesh.shape["blk"]
    x, y = n_head // CORES, n_blk // PLANES
    shape = (x, CORES, 2, PLANES // 2, y)
    wide = Mesh(np.asarray(mesh.devices).reshape(shape), AXES)
    split, gather = (("x", "zl", "y"), ()) if x * y * 2 <= 8 else (("x", "zl"), ("y",))
    spec = P(AXES, None, None)
    return jax.shard_map(
        functools.partial(shards, split, gather),
        mesh=wide,
        in_specs=(spec, spec, spec, P(), P()),
        out_specs=P(AXES, None),
        check_vma=False,
    )
```

```python
import functools
import math

import jax
import jax.numpy as jnp
import numpy as np
from jax import lax
from jax.experimental import pallas as pl
from jax.experimental.pallas import tpu as pltpu
from jax.sharding import Mesh
from jax.sharding import PartitionSpec as P

BLOCK = 128
NEG = -1e30
CORES = 2
PLANES = 4
AXES = ("x", "c", "zh", "zl", "y")
VMEM = pl.BlockSpec(memory_space=pltpu.VMEM)
SMEM = pl.BlockSpec(memory_space=pltpu.SMEM)


def swap(size, bit):
    return [(i, i ^ bit) for i in range(size)]


def after(value, *others):
    return lax.optimization_barrier((value, *others))[0]


def grant(*arrays):
    held = sum(math.prod(a.shape) * a.dtype.itemsize for a in arrays)
    return pltpu.CompilerParams(vmem_limit_bytes=10 * 2**20 + 2 * held)


def bias_kernel(sources, chunk, place_ref, mask_ref, rows_ref, cols_ref, bias_ref):
    tiles, qb, _ = bias_ref.shape
    blocks = mask_ref.shape[1]
    span = cols_ref.shape[1]
    mask = (mask_ref[chunk * tiles * qb + place_ref[sources]] > 0).astype(jnp.bfloat16)
    lanes = lax.broadcasted_iota(jnp.int32, (qb, blocks), 1)
    depth = lax.broadcasted_iota(jnp.int32, (blocks, span), 0)
    rows = []
    for tile in range(tiles):
        mine = (lanes == rows_ref[...] + place_ref[tile]).astype(jnp.bfloat16)
        rows.append(jnp.dot(mine, mask, preferred_element_type=jnp.float32).astype(jnp.bfloat16))
    for n in range(sources):
        pick = (depth == cols_ref[...] + place_ref[n]).astype(jnp.bfloat16)
        for tile in range(tiles):
            seen = jnp.dot(rows[tile], pick, preferred_element_type=jnp.float32)
            bias_ref[tile, :, n * span : (n + 1) * span] = jnp.where(seen > 0.5, 0.0, NEG)


def attend_kernel(picks, count, scale, first, last, place_ref, bias_ref, q_ref, *refs):
    kv_refs, rest = refs[:count], refs[count:]
    if not first:
        m_in, acc_in = rest[:2]
        rest = rest[2:]
    tiles, qb, _ = bias_ref.shape
    block, hdim = q_ref.shape[2:]
    rows = qb * block

    def tile(index, carry):
        q = q_ref[:, 3 * index].reshape(rows, hdim)
        if first:
            m = jnp.full((rows, 1), NEG, jnp.float32)
            acc = jnp.zeros((rows, 2 * hdim), jnp.float32)
        else:
            m = jnp.max(m_in[pl.ds(index * rows, rows), :], axis=1, keepdims=True)
            acc = acc_in[pl.ds(index * rows, rows), :]
        for which, kpart, vpart, source in picks:
            k = kv_refs[which][:, kpart].reshape(rows, hdim)
            v = kv_refs[which][:, vpart].reshape(rows, hdim)
            v = jnp.concatenate([v, jnp.ones((rows, hdim), v.dtype)], axis=1)
            s = lax.dot_general(q, k, (((1,), (1,)), ((), ())), preferred_element_type=jnp.float32)
            bias = bias_ref[index, :, source * rows : (source + 1) * rows]
            s = (s.reshape(qb, block, rows) * scale + bias[:, None, :]).reshape(rows, rows)
            m_next = jnp.maximum(m, jnp.max(s, axis=1, keepdims=True))
            p = jnp.exp2(s - m_next).astype(jnp.bfloat16)
            acc = acc * jnp.exp2(m - m_next) + jnp.dot(p, v, preferred_element_type=jnp.float32)
            m = m_next
        if last:
            out = (acc[:, :hdim] / acc[:, hdim:]).astype(jnp.bfloat16)
            for row in range(qb):
                rest[0][place_ref[index * qb + row]] = out[row * block : (row + 1) * block]
        else:
            rest[0][pl.ds(index * rows, rows), :] = jnp.broadcast_to(m, (rows, hdim))
            rest[1][pl.ds(index * rows, rows), :] = acc
        return carry

    lax.fori_loop(0, tiles, tile, 0)


def attend(place, bias, q, arrays, picks, state, last):
    tiles, qb, _ = bias.shape
    block, hdim = q.shape[2:]
    groups = tiles * qb
    total = groups * block
    first = state is None
    if last:
        out_shape = jax.ShapeDtypeStruct((groups, block, hdim), jnp.bfloat16)
        out_specs = VMEM
    else:
        out_shape = (
            jax.ShapeDtypeStruct((total, hdim), jnp.float32),
            jax.ShapeDtypeStruct((total, 2 * hdim), jnp.float32),
        )
        out_specs = (VMEM, VMEM)
    args = [place, bias, q, *arrays, *(() if first else state)]
    scale = hdim**-0.5 * math.log2(math.e)
    return pl.pallas_call(
        functools.partial(attend_kernel, picks, len(arrays), scale, first, last),
        out_shape=out_shape,
        in_specs=[SMEM] + [VMEM] * (len(args) - 1),
        out_specs=out_specs,
        compiler_params=grant(*args),
        cost_estimate=pl.CostEstimate(flops=total, bytes_accessed=4 * total, transcendentals=0),
    )(*args)


def pack_kernel(takes, *refs):
    at = 0
    for ref, parts in zip(refs, takes):
        for part in parts:
            refs[-1][:, at] = ref[:, part]
            at += 1


def pack(*takes, cost=10**6):
    arrays = [a for a, _ in takes]
    first = arrays[0]
    count = sum(len(parts) for _, parts in takes)
    return pl.pallas_call(
        functools.partial(pack_kernel, [tuple(parts) for _, parts in takes]),
        out_shape=jax.ShapeDtypeStruct((first.shape[0], count) + first.shape[2:], first.dtype),
        in_specs=[VMEM] * len(arrays),
        out_specs=VMEM,
        compiler_params=grant(*arrays),
        cost_estimate=pl.CostEstimate(flops=cost, bytes_accessed=10**4, transcendentals=0),
    )(*arrays)


def finish_kernel(step, part_ref, weight_ref, total_ref, out_ref, rows_ref, sems):
    width = rows_ref.shape[1]
    first = weight_ref.shape[0] - width
    copies = []
    for i in range(rows_ref.shape[0]):
        source = weight_ref.at[first:, i * step : (i + 1) * step]
        copies.append(pltpu.make_async_copy(source, rows_ref.at[i], sems.at[i]))
        copies[i].start()
    joined = jnp.concatenate([part_ref[i] for i in range(part_ref.shape[0])], axis=1)
    for i, copy in enumerate(copies):
        copy.wait()
        at = slice(i * step, (i + 1) * step)
        product = jnp.dot(joined, rows_ref[i], preferred_element_type=jnp.float32)
        out_ref[:, at] = (total_ref[:, at] + product).astype(out_ref.dtype)


def finish(part, weight, total):
    pieces, _, hdim = part.shape
    step = math.gcd(weight.shape[1], 512)
    count = weight.shape[1] // step
    rows = jax.ShapeDtypeStruct((count, pieces * hdim, step), weight.dtype)
    return pl.pallas_call(
        functools.partial(finish_kernel, step),
        out_shape=jax.ShapeDtypeStruct(total.shape, jnp.bfloat16),
        in_specs=[VMEM, pl.BlockSpec(memory_space=pltpu.HBM), VMEM],
        out_specs=VMEM,
        scratch_shapes=[pltpu.VMEM(rows.shape, rows.dtype), pltpu.SemaphoreType.DMA((count,))],
        compiler_params=pltpu.CompilerParams(vmem_limit_bytes=50 * 2**20),
    )(part, weight, total)


def shards(split, gather, queries, keys, values, block_mask, out_weight):
    sizes = {a: lax.axis_size(a) for a in AXES}
    stride = {a: math.prod(list(sizes.values())[i + 1 :]) for i, a in enumerate(AXES)}
    flat = tuple(a for a in split if a != "zl")
    n_split = math.prod(sizes[a] for a in split)
    n_flat = math.prod(sizes[a] for a in flat)
    tok, heads, hdim = queries.shape
    chunks = heads // n_split
    width = n_split * hdim
    here = lax.axis_index("zl")

    order = ("zl", "zh") + gather + ("c",)
    bits = [dict(zip(reversed(order), b)) for b in np.ndindex(*(sizes[a] for a in reversed(order)))]
    sources = len(bits)
    half = sources // 4
    place = sum(
        (lax.axis_index(a) ^ np.array([b[a] for b in bits] + [0], np.int32)) * stride[a] for a in order
    )
    place = jnp.where(np.arange(sources + 1) == sources, lax.axis_index(split), place).astype(jnp.int32)
    local = np.zeros(1, np.int32)
    for a in flat:
        local = (local[:, None] + np.arange(sizes[a], dtype=np.int32) * stride[a]).reshape(-1)
    spot = np.arange(n_split).reshape([sizes[a] for a in split])
    spot = np.moveaxis(spot, split.index("zl"), 0).reshape(2, n_flat).astype(np.int32)
    home = jnp.where(here == 0, spot, spot[::-1]).reshape(-1)

    def across(a, axis, bit):
        n = math.prod(sizes[x] for x in axis) if isinstance(axis, tuple) else sizes[axis]
        return lax.ppermute(a, axis, swap(n, bit))

    def spread(a, axes):
        return lax.all_to_all(a, axes, split_axis=0, concat_axis=0, tiled=True)

    def pieces(arrays, j, bit):
        out = []
        for a in arrays:
            a = jnp.transpose(a[:, j * n_split : (j + 1) * n_split], (1, 0, 2))
            a = a.reshape([sizes[x] for x in split] + [tok, hdim])
            a = lax.dynamic_index_in_dim(a, here ^ bit, split.index("zl"), keepdims=False)
            out.append(a.reshape(n_flat, tok, hdim))
        return jnp.stack(out, axis=1)

    def gathered(array, axes):
        arrays = [array]
        for a in axes:
            arrays = [p if bit == 0 else across(p, a, bit) for bit in range(sizes[a]) for p in arrays]
        return arrays

    out = jax.ShapeDtypeStruct((2, n_flat, sources * n_flat * BLOCK), jnp.float32)

    def bias_of(j, *before):
        return pl.pallas_call(
            functools.partial(bias_kernel, sources, j),
            out_shape=out,
            in_specs=[SMEM, VMEM, VMEM, VMEM],
            out_specs=VMEM,
            compiler_params=grant(out, block_mask),
            cost_estimate=pl.CostEstimate(flops={2: 3 * 10**9, 0: 8 * 10**9, 1: 8 * 10**9}[j], bytes_accessed=0, transcendentals=0),
        )(place, after(block_mask, *before), local[:, None], np.repeat(local, BLOCK)[None, :])

    assert chunks == 3
    trio = (queries, keys, values)

    def cross(j, *before):
        halves = [pieces((keys, values), j, b) for b in range(2)]
        halves = halves[:1] + after(halves[1:], *before) if j == 0 else after(halves, *before)
        return [across(h, ("zh", "zl"), 2 + b) for b, h in enumerate(halves)]

    def own(j, *before):
        given = pieces(trio, j, 1)
        if before:
            given = after(given, *before)
        return (pieces(trio, j, 0), range(3)), (across(given, "zl", 1), range(3))

    near_pick = tuple((i, 2 * r, 2 * r + 1, 4 * i + r) for i in range(half) for r in range(2))
    far_pick = tuple((i, 2 * r, 2 * r + 1, 4 * i + 2 + r) for i in range(half) for r in range(2))
    both_pick = tuple((i, 1 + 3 * r, 2 + 3 * r, 4 * i + r) for i in range(half) for r in range(2))
    both_pick += tuple((i, 6 + 2 * r, 7 + 2 * r, 4 * i + 2 + r) for i in range(half) for r in range(2))
    axes = gather + ("c",)

    own2 = own(2)
    far0 = cross(0, own2[1][0])
    got2 = spread(pack(*own2), flat)
    bias2 = bias_of(2, *far0)
    own0 = pack(*own(0, own2[1][0]), *((f, range(2)) for f in far0))
    got2 = after(got2, bias2, own0)
    kv2 = pack((got2, (1, 2, 4, 5)))
    far1 = cross(1, own2[1][0])
    got0 = spread(after(own0, kv2), flat)
    bias0 = bias_of(0, *far1)
    state2 = attend(home, bias2, got2, gathered(kv2, axes), near_pick, None, False)
    own1 = pack(*own(1, *far0), *((f, range(2)) for f in far1))
    got0 = after(got0, bias0, own1, state2)
    far2 = across(kv2, "zh", 1)
    got1 = spread(after(own1, got0), flat)
    out0 = attend(home, bias0, got0, gathered(got0, axes), both_pick, None, True)
    bias1 = bias_of(1, far2, out0)
    got1 = after(got1, bias1)
    far2 = gathered(far2, axes)
    out1 = attend(home, bias1, got1, gathered(got1, axes), both_pick, None, True)
    ready = jnp.stack([out0, out1], axis=1)
    early = spread(ready, split)
    out2 = attend(home, bias2, got2, far2, far_pick, after(state2, ready), True)
    late = spread(after(out2, early), split)

    rows = 2 * width
    early = jnp.transpose(after(early, out2), (2, 1, 0, 3)).reshape(tok, rows)
    total = jnp.dot(early, out_weight[:rows], preferred_element_type=jnp.float32)
    return finish(late, out_weight, total)


def solution(mesh):
    n_head, n_blk = mesh.shape["head"], mesh.shape["blk"]
    x, y = n_head // CORES, n_blk // PLANES
    shape = (x, CORES, 2, PLANES // 2, y)
    wide = Mesh(np.asarray(mesh.devices).reshape(shape), AXES)
    split, gather = (("x", "zl", "y"), ()) if x * y * 2 <= 8 else (("x", "zl"), ("y",))
    spec = P(AXES, None, None)
    return jax.shard_map(
        functools.partial(shards, split, gather),
        mesh=wide,
        in_specs=(spec, spec, spec, P(), P()),
        out_specs=P(AXES, None),
        check_vma=False,
    )
```

```python
import functools
import math

import jax
import jax.numpy as jnp
import numpy as np
from jax import lax
from jax.experimental import pallas as pl
from jax.experimental.pallas import tpu as pltpu
from jax.sharding import Mesh
from jax.sharding import PartitionSpec as P

BLOCK = 128
NEG = -1e30
CORES = 2
PLANES = 4
AXES = ("x", "c", "zh", "zl", "y")
VMEM = pl.BlockSpec(memory_space=pltpu.VMEM)
SMEM = pl.BlockSpec(memory_space=pltpu.SMEM)


def swap(size, bit):
    return [(i, i ^ bit) for i in range(size)]


def after(value, *others):
    return lax.optimization_barrier((value, *others))[0]


def grant(*arrays):
    held = sum(math.prod(a.shape) * a.dtype.itemsize for a in arrays)
    return pltpu.CompilerParams(vmem_limit_bytes=10 * 2**20 + 2 * held)


def bias_kernel(sources, chunk, place_ref, mask_ref, rows_ref, cols_ref, bias_ref):
    tiles, qb, _ = bias_ref.shape
    blocks = mask_ref.shape[1]
    span = cols_ref.shape[1]
    mask = (mask_ref[chunk * tiles * qb + place_ref[sources]] > 0).astype(jnp.bfloat16)
    lanes = lax.broadcasted_iota(jnp.int32, (qb, blocks), 1)
    depth = lax.broadcasted_iota(jnp.int32, (blocks, span), 0)
    rows = []
    for tile in range(tiles):
        mine = (lanes == rows_ref[...] + place_ref[tile]).astype(jnp.bfloat16)
        rows.append(jnp.dot(mine, mask, preferred_element_type=jnp.float32).astype(jnp.bfloat16))
    for n in range(sources):
        pick = (depth == cols_ref[...] + place_ref[n]).astype(jnp.bfloat16)
        for tile in range(tiles):
            seen = jnp.dot(rows[tile], pick, preferred_element_type=jnp.float32)
            bias_ref[tile, :, n * span : (n + 1) * span] = jnp.where(seen > 0.5, 0.0, NEG)


def attend_kernel(picks, count, scale, place_ref, bias_ref, q_ref, *refs):
    kv_refs, out_ref = refs[:count], refs[count]
    tiles, qb, _ = bias_ref.shape
    block, hdim = q_ref.shape[2:]
    rows = qb * block

    def tile(index, carry):
        q = q_ref[:, 3 * index].reshape(rows, hdim)
        m = jnp.full((rows, 1), NEG, jnp.float32)
        acc = jnp.zeros((rows, 2 * hdim), jnp.float32)
        for which, kpart, vpart, source in picks:
            k = kv_refs[which][:, kpart].reshape(rows, hdim)
            v = kv_refs[which][:, vpart].reshape(rows, hdim)
            v = jnp.concatenate([v, jnp.ones((rows, hdim), v.dtype)], axis=1)
            s = lax.dot_general(q, k, (((1,), (1,)), ((), ())), preferred_element_type=jnp.float32)
            bias = bias_ref[index, :, source * rows : (source + 1) * rows]
            s = (s.reshape(qb, block, rows) * scale + bias[:, None, :]).reshape(rows, rows)
            m_next = jnp.maximum(m, jnp.max(s, axis=1, keepdims=True))
            p = jnp.exp2(s - m_next).astype(jnp.bfloat16)
            acc = acc * jnp.exp2(m - m_next) + jnp.dot(p, v, preferred_element_type=jnp.float32)
            m = m_next
        out = (acc[:, :hdim] / acc[:, hdim:]).astype(jnp.bfloat16)
        for row in range(qb):
            out_ref[place_ref[index * qb + row]] = out[row * block : (row + 1) * block]
        return carry

    lax.fori_loop(0, tiles, tile, 0)


def attend(place, bias, got, arrays, picks):
    tiles, qb, _ = bias.shape
    block, hdim = got.shape[2:]
    groups = tiles * qb
    args = [place, bias, got, *arrays]
    scale = hdim**-0.5 * math.log2(math.e)
    return pl.pallas_call(
        functools.partial(attend_kernel, picks, len(arrays), scale),
        out_shape=jax.ShapeDtypeStruct((groups, block, hdim), jnp.bfloat16),
        in_specs=[SMEM] + [VMEM] * (len(args) - 1),
        out_specs=VMEM,
        compiler_params=grant(*args),
        cost_estimate=pl.CostEstimate(flops=groups * block, bytes_accessed=4 * groups * block, transcendentals=0),
    )(*args)


def pack_kernel(takes, *refs):
    at = 0
    for ref, parts in zip(refs, takes):
        for part in parts:
            refs[-1][:, at] = ref[:, part]
            at += 1


def pack(*takes, cost=10**6):
    arrays = [a for a, _ in takes]
    first = arrays[0]
    count = sum(len(parts) for _, parts in takes)
    return pl.pallas_call(
        functools.partial(pack_kernel, [tuple(parts) for _, parts in takes]),
        out_shape=jax.ShapeDtypeStruct((first.shape[0], count) + first.shape[2:], first.dtype),
        in_specs=[VMEM] * len(arrays),
        out_specs=VMEM,
        compiler_params=grant(*arrays),
        cost_estimate=pl.CostEstimate(flops=cost, bytes_accessed=10**4, transcendentals=0),
    )(*arrays)


def finish_kernel(step, part_ref, weight_ref, total_ref, out_ref, rows_ref, sems):
    width = rows_ref.shape[1]
    first = weight_ref.shape[0] - width
    copies = []
    for i in range(rows_ref.shape[0]):
        source = weight_ref.at[first:, i * step : (i + 1) * step]
        copies.append(pltpu.make_async_copy(source, rows_ref.at[i], sems.at[i]))
        copies[i].start()
    joined = jnp.concatenate([part_ref[i] for i in range(part_ref.shape[0])], axis=1)
    for i, copy in enumerate(copies):
        copy.wait()
        at = slice(i * step, (i + 1) * step)
        product = jnp.dot(joined, rows_ref[i], preferred_element_type=jnp.float32)
        out_ref[:, at] = (total_ref[:, at] + product).astype(out_ref.dtype)


def finish(part, weight, total):
    pieces, _, hdim = part.shape
    step = math.gcd(weight.shape[1], 512)
    count = weight.shape[1] // step
    rows = jax.ShapeDtypeStruct((count, pieces * hdim, step), weight.dtype)
    return pl.pallas_call(
        functools.partial(finish_kernel, step),
        out_shape=jax.ShapeDtypeStruct(total.shape, jnp.bfloat16),
        in_specs=[VMEM, pl.BlockSpec(memory_space=pltpu.HBM), VMEM],
        out_specs=VMEM,
        scratch_shapes=[pltpu.VMEM(rows.shape, rows.dtype), pltpu.SemaphoreType.DMA((count,))],
        compiler_params=pltpu.CompilerParams(vmem_limit_bytes=50 * 2**20),
    )(part, weight, total)


def shards(split, gather, queries, keys, values, block_mask, out_weight):
    sizes = {a: lax.axis_size(a) for a in AXES}
    stride = {a: math.prod(list(sizes.values())[i + 1 :]) for i, a in enumerate(AXES)}
    flat = tuple(a for a in split if a != "zl")
    n_split = math.prod(sizes[a] for a in split)
    n_flat = math.prod(sizes[a] for a in flat)
    tok, heads, hdim = queries.shape
    chunks = heads // n_split
    width = n_split * hdim
    here = lax.axis_index("zl")

    order = ("zl", "zh") + gather + ("c",)
    bits = [dict(zip(reversed(order), b)) for b in np.ndindex(*(sizes[a] for a in reversed(order)))]
    sources = len(bits)
    half = sources // 4
    place = sum(
        (lax.axis_index(a) ^ np.array([b[a] for b in bits] + [0], np.int32)) * stride[a] for a in order
    )
    place = jnp.where(np.arange(sources + 1) == sources, lax.axis_index(split), place).astype(jnp.int32)
    local = np.zeros(1, np.int32)
    for a in flat:
        local = (local[:, None] + np.arange(sizes[a], dtype=np.int32) * stride[a]).reshape(-1)
    spot = np.arange(n_split).reshape([sizes[a] for a in split])
    spot = np.moveaxis(spot, split.index("zl"), 0).reshape(2, n_flat).astype(np.int32)
    home = jnp.where(here == 0, spot, spot[::-1]).reshape(-1)

    def across(a, axis, bit):
        n = math.prod(sizes[x] for x in axis) if isinstance(axis, tuple) else sizes[axis]
        return lax.ppermute(a, axis, swap(n, bit))

    def spread(a, axes):
        return lax.all_to_all(a, axes, split_axis=0, concat_axis=0, tiled=True)

    def pieces(arrays, j, bit):
        out = []
        for a in arrays:
            a = jnp.transpose(a[:, j * n_split : (j + 1) * n_split], (1, 0, 2))
            a = a.reshape([sizes[x] for x in split] + [tok, hdim])
            a = lax.dynamic_index_in_dim(a, here ^ bit, split.index("zl"), keepdims=False)
            out.append(a.reshape(n_flat, tok, hdim))
        return jnp.stack(out, axis=1)

    def gathered(array, axes):
        arrays = [array]
        for a in axes:
            arrays = [p if bit == 0 else across(p, a, bit) for bit in range(sizes[a]) for p in arrays]
        return arrays

    out = jax.ShapeDtypeStruct((2, n_flat, sources * n_flat * BLOCK), jnp.float32)

    def bias_of(j, *before):
        return pl.pallas_call(
            functools.partial(bias_kernel, sources, j),
            out_shape=out,
            in_specs=[SMEM, VMEM, VMEM, VMEM],
            out_specs=VMEM,
            compiler_params=grant(out, block_mask),
            cost_estimate=pl.CostEstimate(flops={2: 10**6, 0: 8 * 10**9, 1: 8 * 10**9}[j], bytes_accessed=0, transcendentals=0),
        )(place, after(block_mask, *before), local[:, None], np.repeat(local, BLOCK)[None, :])

    assert chunks == 3

    def cross(j, *before):
        halves = [pieces((keys, values), j, b) for b in range(2)]
        if before:
            halves = after(halves, *before)
        return [across(h, ("zh", "zl"), 2 + b) for b, h in enumerate(halves)]

    def joined(j, far):
        trio = (queries, keys, values)
        swapped = across(pieces(trio, j, 1), "zl", 1)
        return pack((pieces(trio, j, 0), range(3)), (swapped, range(3)), *((f, range(2)) for f in far))

    picks = tuple((i, 1 + 3 * r, 2 + 3 * r, 4 * i + r) for i in range(half) for r in range(2))
    picks += tuple((i, 6 + 2 * r, 7 + 2 * r, 4 * i + 2 + r) for i in range(half) for r in range(2))
    axes = gather + ("c",)

    far0 = cross(0)
    own0 = joined(0, far0)
    far1 = cross(1, far0[0])
    got0 = spread(own0, flat)
    bias0 = bias_of(0, *far1)
    own1 = joined(1, far1)
    got0 = after(got0, bias0, own1)
    far2 = cross(2, far1[0])
    got1 = spread(after(own1, got0), flat)
    out0 = attend(home, bias0, got0, gathered(got0, axes), picks)
    bias1 = bias_of(1, *far2, out0)
    own2 = joined(2, far2)
    got1 = after(got1, bias1, own2)
    got2 = spread(after(own2, got1), flat)
    bias2 = bias_of(2, bias1)
    out1 = attend(home, bias1, got1, gathered(got1, axes), picks)
    ready = jnp.stack([out0, out1], axis=1)
    got2 = after(got2, ready, bias2)
    early = spread(ready, split)
    out2 = attend(home, bias2, got2, gathered(got2, axes), picks)
    late = spread(out2, split)

    rows = 2 * width
    early = jnp.transpose(after(early, out2), (2, 1, 0, 3)).reshape(tok, rows)
    total = jnp.dot(early, out_weight[:rows], preferred_element_type=jnp.float32)
    return finish(late, out_weight, total)


def solution(mesh):
    n_head, n_blk = mesh.shape["head"], mesh.shape["blk"]
    x, y = n_head // CORES, n_blk // PLANES
    shape = (x, CORES, 2, PLANES // 2, y)
    wide = Mesh(np.asarray(mesh.devices).reshape(shape), AXES)
    split, gather = (("x", "zl", "y"), ()) if x * y * 2 <= 8 else (("x", "zl"), ("y",))
    spec = P(AXES, None, None)
    return jax.shard_map(
        functools.partial(shards, split, gather),
        mesh=wide,
        in_specs=(spec, spec, spec, P(), P()),
        out_specs=P(AXES, None),
        check_vma=False,
    )
```

```python
import functools
import math

import jax
import jax.numpy as jnp
import numpy as np
from jax import lax
from jax.experimental import pallas as pl
from jax.experimental.pallas import tpu as pltpu
from jax.sharding import Mesh
from jax.sharding import PartitionSpec as P

BLOCK = 128
NEG = -1e30
CORES = 2
PLANES = 4
AXES = ("x", "c", "zh", "zl", "y")
VMEM = pl.BlockSpec(memory_space=pltpu.VMEM)
SMEM = pl.BlockSpec(memory_space=pltpu.SMEM)


def swap(size, bit):
    return [(i, i ^ bit) for i in range(size)]


def after(value, *others):
    return lax.optimization_barrier((value, *others))[0]


def grant(*arrays):
    held = sum(math.prod(a.shape) * a.dtype.itemsize for a in arrays)
    return pltpu.CompilerParams(vmem_limit_bytes=10 * 2**20 + 2 * held)


def bias_kernel(sources, chunk, place_ref, mask_ref, rows_ref, cols_ref, bias_ref):
    tiles, qb, _ = bias_ref.shape
    blocks = mask_ref.shape[1]
    span = cols_ref.shape[1]
    mask = (mask_ref[chunk * tiles * qb + place_ref[sources]] > 0).astype(jnp.bfloat16)
    lanes = lax.broadcasted_iota(jnp.int32, (qb, blocks), 1)
    depth = lax.broadcasted_iota(jnp.int32, (blocks, span), 0)
    rows = []
    for tile in range(tiles):
        mine = (lanes == rows_ref[...] + place_ref[tile]).astype(jnp.bfloat16)
        rows.append(jnp.dot(mine, mask, preferred_element_type=jnp.float32).astype(jnp.bfloat16))
    for n in range(sources):
        pick = (depth == cols_ref[...] + place_ref[n]).astype(jnp.bfloat16)
        for tile in range(tiles):
            seen = jnp.dot(rows[tile], pick, preferred_element_type=jnp.float32)
            bias_ref[tile, :, n * span : (n + 1) * span] = jnp.where(seen > 0.5, 0.0, NEG)


def attend_kernel(picks, count, scale, place_ref, bias_ref, q_ref, *refs):
    kv_refs, out_ref = refs[:count], refs[count]
    tiles, qb, _ = bias_ref.shape
    block, hdim = q_ref.shape[2:]
    rows = qb * block

    def tile(index, carry):
        q = q_ref[:, 3 * index].reshape(rows, hdim)
        m = jnp.full((rows, 1), NEG, jnp.float32)
        acc = jnp.zeros((rows, 2 * hdim), jnp.float32)
        for which, kpart, vpart, source in picks:
            k = kv_refs[which][:, kpart].reshape(rows, hdim)
            v = kv_refs[which][:, vpart].reshape(rows, hdim)
            v = jnp.concatenate([v, jnp.ones((rows, hdim), v.dtype)], axis=1)
            s = lax.dot_general(q, k, (((1,), (1,)), ((), ())), preferred_element_type=jnp.float32)
            bias = bias_ref[index, :, source * rows : (source + 1) * rows]
            s = (s.reshape(qb, block, rows) * scale + bias[:, None, :]).reshape(rows, rows)
            m_next = jnp.maximum(m, jnp.max(s, axis=1, keepdims=True))
            p = jnp.exp2(s - m_next).astype(jnp.bfloat16)
            acc = acc * jnp.exp2(m - m_next) + jnp.dot(p, v, preferred_element_type=jnp.float32)
            m = m_next
        out = (acc[:, :hdim] / acc[:, hdim:]).astype(jnp.bfloat16)
        for row in range(qb):
            out_ref[place_ref[index * qb + row]] = out[row * block : (row + 1) * block]
        return carry

    lax.fori_loop(0, tiles, tile, 0)


def attend(place, bias, got, arrays, picks):
    tiles, qb, _ = bias.shape
    block, hdim = got.shape[2:]
    groups = tiles * qb
    args = [place, bias, got, *arrays]
    scale = hdim**-0.5 * math.log2(math.e)
    return pl.pallas_call(
        functools.partial(attend_kernel, picks, len(arrays), scale),
        out_shape=jax.ShapeDtypeStruct((groups, block, hdim), jnp.bfloat16),
        in_specs=[SMEM] + [VMEM] * (len(args) - 1),
        out_specs=VMEM,
        compiler_params=grant(*args),
        cost_estimate=pl.CostEstimate(flops=groups * block, bytes_accessed=4 * groups * block, transcendentals=0),
    )(*args)


def pack_kernel(takes, *refs):
    at = 0
    for ref, parts in zip(refs, takes):
        for part in parts:
            refs[-1][:, at] = ref[:, part]
            at += 1


def pack(*takes, cost=10**6):
    arrays = [a for a, _ in takes]
    first = arrays[0]
    count = sum(len(parts) for _, parts in takes)
    return pl.pallas_call(
        functools.partial(pack_kernel, [tuple(parts) for _, parts in takes]),
        out_shape=jax.ShapeDtypeStruct((first.shape[0], count) + first.shape[2:], first.dtype),
        in_specs=[VMEM] * len(arrays),
        out_specs=VMEM,
        compiler_params=grant(*arrays),
        cost_estimate=pl.CostEstimate(flops=cost, bytes_accessed=10**4, transcendentals=0),
    )(*arrays)


def finish_kernel(step, part_ref, weight_ref, total_ref, out_ref, rows_ref, sems):
    width = rows_ref.shape[1]
    first = weight_ref.shape[0] - width
    copies = []
    for i in range(rows_ref.shape[0]):
        source = weight_ref.at[first:, i * step : (i + 1) * step]
        copies.append(pltpu.make_async_copy(source, rows_ref.at[i], sems.at[i]))
        copies[i].start()
    joined = jnp.concatenate([part_ref[i] for i in range(part_ref.shape[0])], axis=1)
    for i, copy in enumerate(copies):
        copy.wait()
        at = slice(i * step, (i + 1) * step)
        product = jnp.dot(joined, rows_ref[i], preferred_element_type=jnp.float32)
        out_ref[:, at] = (total_ref[:, at] + product).astype(out_ref.dtype)


def finish(part, weight, total):
    pieces, _, hdim = part.shape
    step = math.gcd(weight.shape[1], 512)
    count = weight.shape[1] // step
    rows = jax.ShapeDtypeStruct((count, pieces * hdim, step), weight.dtype)
    return pl.pallas_call(
        functools.partial(finish_kernel, step),
        out_shape=jax.ShapeDtypeStruct(total.shape, jnp.bfloat16),
        in_specs=[VMEM, pl.BlockSpec(memory_space=pltpu.HBM), VMEM],
        out_specs=VMEM,
        scratch_shapes=[pltpu.VMEM(rows.shape, rows.dtype), pltpu.SemaphoreType.DMA((count,))],
        compiler_params=pltpu.CompilerParams(vmem_limit_bytes=50 * 2**20),
    )(part, weight, total)


def shards(split, gather, queries, keys, values, block_mask, out_weight):
    sizes = {a: lax.axis_size(a) for a in AXES}
    stride = {a: math.prod(list(sizes.values())[i + 1 :]) for i, a in enumerate(AXES)}
    flat = tuple(a for a in split if a != "zl")
    n_split = math.prod(sizes[a] for a in split)
    n_flat = math.prod(sizes[a] for a in flat)
    tok, heads, hdim = queries.shape
    chunks = heads // n_split
    width = n_split * hdim
    here = lax.axis_index("zl")

    order = ("zl", "zh") + gather + ("c",)
    bits = [dict(zip(reversed(order), b)) for b in np.ndindex(*(sizes[a] for a in reversed(order)))]
    sources = len(bits)
    half = sources // 4
    place = sum(
        (lax.axis_index(a) ^ np.array([b[a] for b in bits] + [0], np.int32)) * stride[a] for a in order
    )
    place = jnp.where(np.arange(sources + 1) == sources, lax.axis_index(split), place).astype(jnp.int32)
    local = np.zeros(1, np.int32)
    for a in flat:
        local = (local[:, None] + np.arange(sizes[a], dtype=np.int32) * stride[a]).reshape(-1)
    spot = np.arange(n_split).reshape([sizes[a] for a in split])
    spot = np.moveaxis(spot, split.index("zl"), 0).reshape(2, n_flat).astype(np.int32)
    home = jnp.where(here == 0, spot, spot[::-1]).reshape(-1)

    def across(a, axis, bit):
        n = math.prod(sizes[x] for x in axis) if isinstance(axis, tuple) else sizes[axis]
        return lax.ppermute(a, axis, swap(n, bit))

    def spread(a, axes):
        return lax.all_to_all(a, axes, split_axis=0, concat_axis=0, tiled=True)

    def pieces(arrays, j, bit):
        out = []
        for a in arrays:
            a = jnp.transpose(a[:, j * n_split : (j + 1) * n_split], (1, 0, 2))
            a = a.reshape([sizes[x] for x in split] + [tok, hdim])
            a = lax.dynamic_index_in_dim(a, here ^ bit, split.index("zl"), keepdims=False)
            out.append(a.reshape(n_flat, tok, hdim))
        return jnp.stack(out, axis=1)

    def gathered(array, axes):
        arrays = [array]
        for a in axes:
            arrays = [p if bit == 0 else across(p, a, bit) for bit in range(sizes[a]) for p in arrays]
        return arrays

    out = jax.ShapeDtypeStruct((2, n_flat, sources * n_flat * BLOCK), jnp.float32)

    def bias_of(j, *before):
        return pl.pallas_call(
            functools.partial(bias_kernel, sources, j),
            out_shape=out,
            in_specs=[SMEM, VMEM, VMEM, VMEM],
            out_specs=VMEM,
            compiler_params=grant(out, block_mask),
            cost_estimate=pl.CostEstimate(flops={2: 10**6, 0: 8 * 10**9, 1: 8 * 10**9}[j], bytes_accessed=0, transcendentals=0),
        )(place, after(block_mask, *before), local[:, None], np.repeat(local, BLOCK)[None, :])

    assert chunks == 3

    trio = (queries, keys, values)

    def halves(j):
        return [pieces((keys, values), j, b) for b in range(2)]

    def cross(held):
        return [across(h, ("zh", "zl"), 2 + b) for b, h in enumerate(held)]

    def plane(j, *before):
        given = pieces(trio, j, 1)
        return pieces(trio, j, 0), across(after(given, *before) if before else given, "zl", 1)

    def joined(own, far):
        return pack(*((a, range(3)) for a in own), *((a, range(2)) for a in far))

    picks = tuple((i, 1 + 3 * r, 2 + 3 * r, 4 * i + r) for i in range(half) for r in range(2))
    picks += tuple((i, 6 + 2 * r, 7 + 2 * r, 4 * i + 2 + r) for i in range(half) for r in range(2))
    axes = gather + ("c",)

    far0 = cross(halves(0))
    plane0 = plane(0)
    own0 = joined(plane0, far0)
    far1 = cross(after(halves(1), far0[0]))
    got0 = spread(own0, flat)
    next2, plane1, plane2 = halves(2), plane(1), plane(2, far0[0])
    bias0 = bias_of(0, *far1, *next2, *plane2)
    own1 = joined(plane1, far1)
    got0 = after(got0, bias0, own1)
    far2 = cross(after(next2, bias0))
    got1 = spread(after(own1, got0), flat)
    out0 = attend(home, bias0, got0, gathered(got0, axes), picks)
    far2 = after(far2, out0)
    bias1 = bias_of(1, *far2)
    own2 = joined(plane2, far2)
    got1 = after(got1, bias1, own2)
    got2 = spread(after(own2, got1), flat)
    bias2 = bias_of(2, bias1)
    out1 = attend(home, bias1, got1, gathered(got1, axes), picks)
    ready = jnp.stack([out0, out1], axis=1)
    got2 = after(got2, ready, bias2)
    early = spread(ready, split)
    out2 = attend(home, bias2, got2, gathered(got2, axes), picks)
    late = spread(out2, split)

    rows = 2 * width
    early = jnp.transpose(after(early, out2), (2, 1, 0, 3)).reshape(tok, rows)
    total = jnp.dot(early, out_weight[:rows], preferred_element_type=jnp.float32)
    return finish(late, out_weight, total)


def solution(mesh):
    n_head, n_blk = mesh.shape["head"], mesh.shape["blk"]
    x, y = n_head // CORES, n_blk // PLANES
    shape = (x, CORES, 2, PLANES // 2, y)
    wide = Mesh(np.asarray(mesh.devices).reshape(shape), AXES)
    split, gather = (("x", "zl", "y"), ()) if x * y * 2 <= 8 else (("x", "zl"), ("y",))
    spec = P(AXES, None, None)
    return jax.shard_map(
        functools.partial(shards, split, gather),
        mesh=wide,
        in_specs=(spec, spec, spec, P(), P()),
        out_specs=P(AXES, None),
        check_vma=False,
    )
```

```python
import functools
import math

import jax
import jax.numpy as jnp
import numpy as np
from jax import lax
from jax.experimental import pallas as pl
from jax.experimental.pallas import tpu as pltpu
from jax.sharding import Mesh
from jax.sharding import PartitionSpec as P

BLOCK = 128
NEG = -1e30
CORES = 2
PLANES = 4
AXES = ("x", "c", "zh", "zl", "y")
VMEM = pl.BlockSpec(memory_space=pltpu.VMEM)
SMEM = pl.BlockSpec(memory_space=pltpu.SMEM)


def swap(size, bit):
    return [(i, i ^ bit) for i in range(size)]


def after(value, *others):
    return lax.optimization_barrier((value, *others))[0]


def grant(*arrays):
    held = sum(math.prod(a.shape) * a.dtype.itemsize for a in arrays)
    return pltpu.CompilerParams(vmem_limit_bytes=10 * 2**20 + 2 * held)


def bias_kernel(sources, chunk, place_ref, mask_ref, rows_ref, cols_ref, bias_ref):
    tiles, qb, _ = bias_ref.shape
    blocks = mask_ref.shape[1]
    span = cols_ref.shape[1]
    mask = (mask_ref[chunk * tiles * qb + place_ref[sources]] > 0).astype(jnp.bfloat16)
    lanes = lax.broadcasted_iota(jnp.int32, (qb, blocks), 1)
    depth = lax.broadcasted_iota(jnp.int32, (blocks, span), 0)
    rows = []
    for tile in range(tiles):
        mine = (lanes == rows_ref[...] + place_ref[tile]).astype(jnp.bfloat16)
        rows.append(jnp.dot(mine, mask, preferred_element_type=jnp.float32).astype(jnp.bfloat16))
    for n in range(sources):
        pick = (depth == cols_ref[...] + place_ref[n]).astype(jnp.bfloat16)
        for tile in range(tiles):
            seen = jnp.dot(rows[tile], pick, preferred_element_type=jnp.float32)
            bias_ref[tile, :, n * span : (n + 1) * span] = jnp.where(seen > 0.5, 0.0, NEG)


def attend_kernel(picks, count, scale, first, last, place_ref, bias_ref, q_ref, *refs):
    kv_refs, rest = refs[:count], refs[count:]
    if not first:
        m_in, acc_in = rest[:2]
        rest = rest[2:]
    tiles, qb, _ = bias_ref.shape
    block, hdim = q_ref.shape[2:]
    rows = qb * block

    def tile(index, carry):
        q = q_ref[:, 3 * index].reshape(rows, hdim)
        if first:
            m = jnp.full((rows, 1), NEG, jnp.float32)
            acc = jnp.zeros((rows, 2 * hdim), jnp.float32)
        else:
            m = jnp.max(m_in[pl.ds(index * rows, rows), :], axis=1, keepdims=True)
            acc = acc_in[pl.ds(index * rows, rows), :]
        for which, kpart, vpart, source in picks:
            k = kv_refs[which][:, kpart].reshape(rows, hdim)
            v = kv_refs[which][:, vpart].reshape(rows, hdim)
            v = jnp.concatenate([v, jnp.ones((rows, hdim), v.dtype)], axis=1)
            s = lax.dot_general(q, k, (((1,), (1,)), ((), ())), preferred_element_type=jnp.float32)
            bias = bias_ref[index, :, source * rows : (source + 1) * rows]
            s = (s.reshape(qb, block, rows) * scale + bias[:, None, :]).reshape(rows, rows)
            m_next = jnp.maximum(m, jnp.max(s, axis=1, keepdims=True))
            p = jnp.exp2(s - m_next).astype(jnp.bfloat16)
            acc = acc * jnp.exp2(m - m_next) + jnp.dot(p, v, preferred_element_type=jnp.float32)
            m = m_next
        if last:
            out = (acc[:, :hdim] / acc[:, hdim:]).astype(jnp.bfloat16)
            for row in range(qb):
                rest[0][place_ref[index * qb + row]] = out[row * block : (row + 1) * block]
        else:
            rest[0][pl.ds(index * rows, rows), :] = jnp.broadcast_to(m, (rows, hdim))
            rest[1][pl.ds(index * rows, rows), :] = acc
        return carry

    lax.fori_loop(0, tiles, tile, 0)


def attend(place, bias, q, arrays, picks, state, last):
    tiles, qb, _ = bias.shape
    block, hdim = q.shape[2:]
    groups = tiles * qb
    total = groups * block
    first = state is None
    if last:
        out_shape = jax.ShapeDtypeStruct((groups, block, hdim), jnp.bfloat16)
        out_specs = VMEM
    else:
        out_shape = (
            jax.ShapeDtypeStruct((total, hdim), jnp.float32),
            jax.ShapeDtypeStruct((total, 2 * hdim), jnp.float32),
        )
        out_specs = (VMEM, VMEM)
    args = [place, bias, q, *arrays, *(() if first else state)]
    scale = hdim**-0.5 * math.log2(math.e)
    return pl.pallas_call(
        functools.partial(attend_kernel, picks, len(arrays), scale, first, last),
        out_shape=out_shape,
        in_specs=[SMEM] + [VMEM] * (len(args) - 1),
        out_specs=out_specs,
        compiler_params=grant(*args),
        cost_estimate=pl.CostEstimate(flops=total, bytes_accessed=4 * total, transcendentals=0),
    )(*args)


def pack_kernel(takes, *refs):
    at = 0
    for ref, parts in zip(refs, takes):
        for part in parts:
            refs[-1][:, at] = ref[:, part]
            at += 1


def pack(*takes, cost=10**6):
    arrays = [a for a, _ in takes]
    first = arrays[0]
    count = sum(len(parts) for _, parts in takes)
    return pl.pallas_call(
        functools.partial(pack_kernel, [tuple(parts) for _, parts in takes]),
        out_shape=jax.ShapeDtypeStruct((first.shape[0], count) + first.shape[2:], first.dtype),
        in_specs=[VMEM] * len(arrays),
        out_specs=VMEM,
        compiler_params=grant(*arrays),
        cost_estimate=pl.CostEstimate(flops=cost, bytes_accessed=10**4, transcendentals=0),
    )(*arrays)


def finish_kernel(step, part_ref, weight_ref, total_ref, out_ref, rows_ref, sems):
    width = rows_ref.shape[1]
    first = weight_ref.shape[0] - width
    copies = []
    for i in range(rows_ref.shape[0]):
        source = weight_ref.at[first:, i * step : (i + 1) * step]
        copies.append(pltpu.make_async_copy(source, rows_ref.at[i], sems.at[i]))
        copies[i].start()
    joined = jnp.concatenate([part_ref[i] for i in range(part_ref.shape[0])], axis=1)
    for i, copy in enumerate(copies):
        copy.wait()
        at = slice(i * step, (i + 1) * step)
        product = jnp.dot(joined, rows_ref[i], preferred_element_type=jnp.float32)
        out_ref[:, at] = (total_ref[:, at] + product).astype(out_ref.dtype)


def finish(part, weight, total):
    pieces, _, hdim = part.shape
    step = math.gcd(weight.shape[1], 512)
    count = weight.shape[1] // step
    rows = jax.ShapeDtypeStruct((count, pieces * hdim, step), weight.dtype)
    return pl.pallas_call(
        functools.partial(finish_kernel, step),
        out_shape=jax.ShapeDtypeStruct(total.shape, jnp.bfloat16),
        in_specs=[VMEM, pl.BlockSpec(memory_space=pltpu.HBM), VMEM],
        out_specs=VMEM,
        scratch_shapes=[pltpu.VMEM(rows.shape, rows.dtype), pltpu.SemaphoreType.DMA((count,))],
        compiler_params=pltpu.CompilerParams(vmem_limit_bytes=50 * 2**20),
    )(part, weight, total)


def shards(split, gather, queries, keys, values, block_mask, out_weight):
    sizes = {a: lax.axis_size(a) for a in AXES}
    stride = {a: math.prod(list(sizes.values())[i + 1 :]) for i, a in enumerate(AXES)}
    flat = tuple(a for a in split if a != "zl")
    n_split = math.prod(sizes[a] for a in split)
    n_flat = math.prod(sizes[a] for a in flat)
    tok, heads, hdim = queries.shape
    chunks = heads // n_split
    width = n_split * hdim
    here = lax.axis_index("zl")

    order = ("zl", "zh") + gather + ("c",)
    bits = [dict(zip(reversed(order), b)) for b in np.ndindex(*(sizes[a] for a in reversed(order)))]
    sources = len(bits)
    half = sources // 4
    place = sum(
        (lax.axis_index(a) ^ np.array([b[a] for b in bits] + [0], np.int32)) * stride[a] for a in order
    )
    place = jnp.where(np.arange(sources + 1) == sources, lax.axis_index(split), place).astype(jnp.int32)
    local = np.zeros(1, np.int32)
    for a in flat:
        local = (local[:, None] + np.arange(sizes[a], dtype=np.int32) * stride[a]).reshape(-1)
    spot = np.arange(n_split).reshape([sizes[a] for a in split])
    spot = np.moveaxis(spot, split.index("zl"), 0).reshape(2, n_flat).astype(np.int32)
    home = jnp.where(here == 0, spot, spot[::-1]).reshape(-1)

    def across(a, axis, bit):
        n = math.prod(sizes[x] for x in axis) if isinstance(axis, tuple) else sizes[axis]
        return lax.ppermute(a, axis, swap(n, bit))

    def spread(a, axes):
        return lax.all_to_all(a, axes, split_axis=0, concat_axis=0, tiled=True)

    def pieces(arrays, j, bit):
        out = []
        for a in arrays:
            a = jnp.transpose(a[:, j * n_split : (j + 1) * n_split], (1, 0, 2))
            a = a.reshape([sizes[x] for x in split] + [tok, hdim])
            a = lax.dynamic_index_in_dim(a, here ^ bit, split.index("zl"), keepdims=False)
            out.append(a.reshape(n_flat, tok, hdim))
        return jnp.stack(out, axis=1)

    def gathered(array, axes):
        arrays = [array]
        for a in axes:
            arrays = [p if bit == 0 else across(p, a, bit) for bit in range(sizes[a]) for p in arrays]
        return arrays

    out = jax.ShapeDtypeStruct((2, n_flat, sources * n_flat * BLOCK), jnp.float32)

    def bias_of(j, *before):
        return pl.pallas_call(
            functools.partial(bias_kernel, sources, j),
            out_shape=out,
            in_specs=[SMEM, VMEM, VMEM, VMEM],
            out_specs=VMEM,
            compiler_params=grant(out, block_mask),
            cost_estimate=pl.CostEstimate(flops=3 * 10**9 if j else 8 * 10**9, bytes_accessed=0, transcendentals=0),
        )(place, after(block_mask, *before), local[:, None], np.repeat(local, BLOCK)[None, :])

    far0 = [across(pieces((keys, values), 0, b), ("zh", "zl"), 2 + b) for b in range(2)]
    trio = (queries, keys, values)
    own = []
    for j in (1, 2, 0) if chunks == 3 else range(chunks):
        own.append((j, pieces(trio, j, 0), across(pieces(trio, j, 1), "zl", 1)))
    last = own[-1]
    own = {j: jnp.concatenate([mine, got], axis=1) for j, mine, got in own[:-1]}

    near_pick = tuple((i, 2 * r, 2 * r + 1, 4 * i + r) for i in range(half) for r in range(2))
    far_pick = tuple((i, 2 * r, 2 * r + 1, 4 * i + 2 + r) for i in range(half) for r in range(2))
    both_pick = tuple((i, 1 + 3 * r, 2 + 3 * r, 4 * i + r) for i in range(half) for r in range(2))
    both_pick += tuple((i, 6 + 2 * r, 7 + 2 * r, 4 * i + 2 + r) for i in range(half) for r in range(2))
    axes = gather + ("c",)
    outs = [None] * chunks
    waiting = []
    far, gate = far0, ()
    for j in range(1, chunks):
        got = spread(after(own[j], *gate), flat)
        bias = bias_of(j, far)
        got = after(got, bias)
        kv = jnp.concatenate([got[:, 1:3], got[:, 4:6]], axis=1)
        gate = (kv,)
        far = across(kv, "zh", 1)
        near = gathered(kv, axes)
        state = attend(home, bias, got, near, near_pick, None, False)
        waiting.append((bias, got, far, state))
    parts = [(a, range(a.shape[1])) for a in (*last[1:], *far0)]
    got = spread(after(pack(*parts), kv), flat)
    for j, (bias, mine, far, state) in enumerate(waiting[:-1], 1):
        outs[j] = attend(home, bias, mine, gathered(far, axes), far_pick, state, True)
    bias, mine, far, state = waiting[-1]
    bias0 = bias_of(0, far)
    got = after(got, bias0, state, outs[-2])
    all0 = gathered(got, axes)
    far_all = gathered(far, axes)
    outs[0] = attend(home, bias0, after(got, *far_all), all0, both_pick, None, True)
    ready = jnp.stack(outs[:-1], axis=1)
    early = spread(ready, split)
    outs[-1] = attend(home, bias, mine, far_all, far_pick, after(state, ready), True)
    late = spread(outs[-1], split)

    rows = (chunks - 1) * width
    early = jnp.transpose(after(early, outs[-1]), (2, 1, 0, 3)).reshape(tok, rows)
    total = jnp.dot(early, out_weight[:rows], preferred_element_type=jnp.float32)
    return finish(late, out_weight, total)


def solution(mesh):
    n_head, n_blk = mesh.shape["head"], mesh.shape["blk"]
    x, y = n_head // CORES, n_blk // PLANES
    shape = (x, CORES, 2, PLANES // 2, y)
    wide = Mesh(np.asarray(mesh.devices).reshape(shape), AXES)
    split, gather = (("x", "zl", "y"), ()) if x * y * 2 <= 8 else (("x", "zl"), ("y",))
    spec = P(AXES, None, None)
    return jax.shard_map(
        functools.partial(shards, split, gather),
        mesh=wide,
        in_specs=(spec, spec, spec, P(), P()),
        out_specs=P(AXES, None),
        check_vma=False,
    )
```

```python
import functools
import math

import jax
import jax.numpy as jnp
import numpy as np
from jax import lax
from jax.experimental import pallas as pl
from jax.experimental.pallas import tpu as pltpu
from jax.sharding import Mesh
from jax.sharding import PartitionSpec as P

BLOCK = 128
NEG = -1e30
CORES = 2
PLANES = 4
AXES = ("x", "c", "zh", "zl", "y")
VMEM = pl.BlockSpec(memory_space=pltpu.VMEM)
SMEM = pl.BlockSpec(memory_space=pltpu.SMEM)


def swap(size, bit):
    return [(i, i ^ bit) for i in range(size)]


def after(value, *others):
    return lax.optimization_barrier((value, *others))[0]


def grant(*arrays):
    held = sum(math.prod(a.shape) * a.dtype.itemsize for a in arrays)
    return pltpu.CompilerParams(vmem_limit_bytes=10 * 2**20 + 2 * held)


def bias_kernel(sources, chunk, place_ref, mask_ref, rows_ref, cols_ref, bias_ref):
    tiles, qb, _ = bias_ref.shape
    blocks = mask_ref.shape[1]
    span = cols_ref.shape[1]
    mask = (mask_ref[chunk * tiles * qb + place_ref[sources]] > 0).astype(jnp.bfloat16)
    lanes = lax.broadcasted_iota(jnp.int32, (qb, blocks), 1)
    depth = lax.broadcasted_iota(jnp.int32, (blocks, span), 0)
    rows = []
    for tile in range(tiles):
        mine = (lanes == rows_ref[...] + place_ref[tile]).astype(jnp.bfloat16)
        rows.append(jnp.dot(mine, mask, preferred_element_type=jnp.float32).astype(jnp.bfloat16))
    for n in range(sources):
        pick = (depth == cols_ref[...] + place_ref[n]).astype(jnp.bfloat16)
        for tile in range(tiles):
            seen = jnp.dot(rows[tile], pick, preferred_element_type=jnp.float32)
            bias_ref[tile, :, n * span : (n + 1) * span] = jnp.where(seen > 0.5, 0.0, NEG)


def attend_kernel(picks, count, extra, scale, first, last, place_ref, bias_ref, q_ref, *refs):
    kv_refs, rest = refs[:count], refs[count:]
    if not first:
        m_in, acc_in = rest[:2]
        rest = rest[2:]
    others, rest = rest[:extra], rest[extra:]
    for i, other in enumerate(others):
        rest[0][:, 1 + i] = other[...]
    tiles, qb, _ = bias_ref.shape
    block, hdim = q_ref.shape[2:]
    rows = qb * block

    def tile(index, carry):
        q = q_ref[:, 3 * index].reshape(rows, hdim)
        if first:
            m = jnp.full((rows, 1), NEG, jnp.float32)
            acc = jnp.zeros((rows, 2 * hdim), jnp.float32)
        else:
            m = jnp.max(m_in[pl.ds(index * rows, rows), :], axis=1, keepdims=True)
            acc = acc_in[pl.ds(index * rows, rows), :]
        for which, kpart, vpart, source in picks:
            k = kv_refs[which][:, kpart].reshape(rows, hdim)
            v = kv_refs[which][:, vpart].reshape(rows, hdim)
            v = jnp.concatenate([v, jnp.ones((rows, hdim), v.dtype)], axis=1)
            s = lax.dot_general(q, k, (((1,), (1,)), ((), ())), preferred_element_type=jnp.float32)
            bias = bias_ref[index, :, source * rows : (source + 1) * rows]
            s = (s.reshape(qb, block, rows) * scale + bias[:, None, :]).reshape(rows, rows)
            m_next = jnp.maximum(m, jnp.max(s, axis=1, keepdims=True))
            p = jnp.exp2(s - m_next).astype(jnp.bfloat16)
            acc = acc * jnp.exp2(m - m_next) + jnp.dot(p, v, preferred_element_type=jnp.float32)
            m = m_next
        if last:
            out = (acc[:, :hdim] / acc[:, hdim:]).astype(jnp.bfloat16)
            for row in range(qb):
                at = place_ref[index * qb + row]
                rest[0][(at, 0) if extra else at] = out[row * block : (row + 1) * block]
        else:
            rest[0][pl.ds(index * rows, rows), :] = jnp.broadcast_to(m, (rows, hdim))
            rest[1][pl.ds(index * rows, rows), :] = acc
        return carry

    lax.fori_loop(0, tiles, tile, 0)


def attend(place, bias, q, arrays, picks, state, last, beside=()):
    tiles, qb, _ = bias.shape
    block, hdim = q.shape[2:]
    groups = tiles * qb
    total = groups * block
    first = state is None
    if last:
        held = (groups, 1 + len(beside), block, hdim) if beside else (groups, block, hdim)
        out_shape = jax.ShapeDtypeStruct(held, jnp.bfloat16)
        out_specs = VMEM
    else:
        out_shape = (
            jax.ShapeDtypeStruct((total, hdim), jnp.float32),
            jax.ShapeDtypeStruct((total, 2 * hdim), jnp.float32),
        )
        out_specs = (VMEM, VMEM)
    args = [place, bias, q, *arrays, *(() if first else state), *beside]
    scale = hdim**-0.5 * math.log2(math.e)
    return pl.pallas_call(
        functools.partial(attend_kernel, picks, len(arrays), len(beside), scale, first, last),
        out_shape=out_shape,
        in_specs=[SMEM] + [VMEM] * (len(args) - 1),
        out_specs=out_specs,
        compiler_params=grant(*args),
        cost_estimate=pl.CostEstimate(flops=total, bytes_accessed=4 * total, transcendentals=0),
    )(*args)


def pack_kernel(takes, *refs):
    at = 0
    for ref, parts in zip(refs, takes):
        for part in parts:
            refs[-1][:, at] = ref[:, part]
            at += 1


def pack(*takes, cost=10**6):
    arrays = [a for a, _ in takes]
    first = arrays[0]
    count = sum(len(parts) for _, parts in takes)
    return pl.pallas_call(
        functools.partial(pack_kernel, [tuple(parts) for _, parts in takes]),
        out_shape=jax.ShapeDtypeStruct((first.shape[0], count) + first.shape[2:], first.dtype),
        in_specs=[VMEM] * len(arrays),
        out_specs=VMEM,
        compiler_params=grant(*arrays),
        cost_estimate=pl.CostEstimate(flops=cost, bytes_accessed=10**4, transcendentals=0),
    )(*arrays)


def finish_kernel(step, part_ref, weight_ref, total_ref, out_ref, rows_ref, sems):
    width = rows_ref.shape[1]
    first = weight_ref.shape[0] - width
    copies = []
    for i in range(rows_ref.shape[0]):
        source = weight_ref.at[first:, i * step : (i + 1) * step]
        copies.append(pltpu.make_async_copy(source, rows_ref.at[i], sems.at[i]))
        copies[i].start()
    joined = jnp.concatenate([part_ref[i] for i in range(part_ref.shape[0])], axis=1)
    for i, copy in enumerate(copies):
        copy.wait()
        at = slice(i * step, (i + 1) * step)
        product = jnp.dot(joined, rows_ref[i], preferred_element_type=jnp.float32)
        out_ref[:, at] = (total_ref[:, at] + product).astype(out_ref.dtype)


def finish(part, weight, total):
    pieces, _, hdim = part.shape
    step = math.gcd(weight.shape[1], 512)
    count = weight.shape[1] // step
    rows = jax.ShapeDtypeStruct((count, pieces * hdim, step), weight.dtype)
    return pl.pallas_call(
        functools.partial(finish_kernel, step),
        out_shape=jax.ShapeDtypeStruct(total.shape, jnp.bfloat16),
        in_specs=[VMEM, pl.BlockSpec(memory_space=pltpu.HBM), VMEM],
        out_specs=VMEM,
        scratch_shapes=[pltpu.VMEM(rows.shape, rows.dtype), pltpu.SemaphoreType.DMA((count,))],
        compiler_params=pltpu.CompilerParams(vmem_limit_bytes=50 * 2**20),
    )(part, weight, total)


def shards(split, gather, queries, keys, values, block_mask, out_weight):
    sizes = {a: lax.axis_size(a) for a in AXES}
    stride = {a: math.prod(list(sizes.values())[i + 1 :]) for i, a in enumerate(AXES)}
    flat = tuple(a for a in split if a != "zl")
    n_split = math.prod(sizes[a] for a in split)
    n_flat = math.prod(sizes[a] for a in flat)
    tok, heads, hdim = queries.shape
    chunks = heads // n_split
    width = n_split * hdim
    here = lax.axis_index("zl")

    order = ("zl", "zh") + gather + ("c",)
    bits = [dict(zip(reversed(order), b)) for b in np.ndindex(*(sizes[a] for a in reversed(order)))]
    sources = len(bits)
    half = sources // 4
    place = sum(
        (lax.axis_index(a) ^ np.array([b[a] for b in bits] + [0], np.int32)) * stride[a] for a in order
    )
    place = jnp.where(np.arange(sources + 1) == sources, lax.axis_index(split), place).astype(jnp.int32)
    local = np.zeros(1, np.int32)
    for a in flat:
        local = (local[:, None] + np.arange(sizes[a], dtype=np.int32) * stride[a]).reshape(-1)
    spot = np.arange(n_split).reshape([sizes[a] for a in split])
    spot = np.moveaxis(spot, split.index("zl"), 0).reshape(2, n_flat).astype(np.int32)
    home = jnp.where(here == 0, spot, spot[::-1]).reshape(-1)

    def across(a, axis, bit):
        n = math.prod(sizes[x] for x in axis) if isinstance(axis, tuple) else sizes[axis]
        return lax.ppermute(a, axis, swap(n, bit))

    def spread(a, axes):
        return lax.all_to_all(a, axes, split_axis=0, concat_axis=0, tiled=True)

    def pieces(arrays, j, bit):
        out = []
        for a in arrays:
            a = jnp.transpose(a[:, j * n_split : (j + 1) * n_split], (1, 0, 2))
            a = a.reshape([sizes[x] for x in split] + [tok, hdim])
            a = lax.dynamic_index_in_dim(a, here ^ bit, split.index("zl"), keepdims=False)
            out.append(a.reshape(n_flat, tok, hdim))
        return jnp.stack(out, axis=1)

    def gathered(array, axes):
        arrays = [array]
        for a in axes:
            arrays = [p if bit == 0 else across(p, a, bit) for bit in range(sizes[a]) for p in arrays]
        return arrays

    out = jax.ShapeDtypeStruct((2, n_flat, sources * n_flat * BLOCK), jnp.float32)

    def bias_of(j, *before):
        return pl.pallas_call(
            functools.partial(bias_kernel, sources, j),
            out_shape=out,
            in_specs=[SMEM, VMEM, VMEM, VMEM],
            out_specs=VMEM,
            compiler_params=grant(out, block_mask),
            cost_estimate=pl.CostEstimate(flops=3 * 10**9 if j else 8 * 10**9, bytes_accessed=0, transcendentals=0),
        )(place, after(block_mask, *before), local[:, None], np.repeat(local, BLOCK)[None, :])

    far0 = [across(pieces((keys, values), 0, b), ("zh", "zl"), 2 + b) for b in range(2)]
    trio = (queries, keys, values)
    own = []
    for j in (1, 2, 0) if chunks == 3 else range(chunks):
        own.append((j, pieces(trio, j, 0), across(pieces(trio, j, 1), "zl", 1)))
    last = own[-1]
    own = {j: jnp.concatenate([mine, got], axis=1) for j, mine, got in own[:-1]}

    near_pick = tuple((i, 2 * r, 2 * r + 1, 4 * i + r) for i in range(half) for r in range(2))
    far_pick = tuple((i, 2 * r, 2 * r + 1, 4 * i + 2 + r) for i in range(half) for r in range(2))
    both_pick = tuple((i, 1 + 3 * r, 2 + 3 * r, 4 * i + r) for i in range(half) for r in range(2))
    both_pick += tuple((i, 6 + 2 * r, 7 + 2 * r, 4 * i + 2 + r) for i in range(half) for r in range(2))
    axes = gather + ("c",)
    outs = [None] * chunks
    waiting = []
    far, gate = far0, ()
    for j in range(1, chunks):
        got = spread(after(own[j], *gate), flat)
        bias = bias_of(j, far)
        if j == chunks - 1:
            packed = pack(*((a, range(a.shape[1])) for a in (*last[1:], *far0)))
            got = after(got, packed)
        got = after(got, bias)
        kv = jnp.concatenate([got[:, 1:3], got[:, 4:6]], axis=1)
        gate = (kv,)
        far = across(kv, "zh", 1)
        near = gathered(kv, axes)
        state = attend(home, bias, got, near, near_pick, None, False)
        waiting.append((bias, got, far, state))
    got = spread(after(packed, kv), flat)
    for j, (bias, mine, far, state) in enumerate(waiting[:-1], 1):
        outs[j] = attend(home, bias, mine, gathered(far, axes), far_pick, state, True)
    bias, mine, far, state = waiting[-1]
    bias0 = bias_of(0, far)
    got = after(got, bias0, state, outs[-2])
    all0 = gathered(got, axes)
    far_all = gathered(far, axes)
    ready = attend(home, bias0, after(got, *far_all), all0, both_pick, None, True, outs[1:-1])
    early = spread(ready, split)
    outs[-1] = attend(home, bias, mine, far_all, far_pick, after(state, ready), True)
    late = spread(outs[-1], split)

    rows = (chunks - 1) * width
    early = jnp.transpose(after(early, outs[-1]), (2, 1, 0, 3)).reshape(tok, rows)
    total = jnp.dot(early, out_weight[:rows], preferred_element_type=jnp.float32)
    return finish(late, out_weight, total)


def solution(mesh):
    n_head, n_blk = mesh.shape["head"], mesh.shape["blk"]
    x, y = n_head // CORES, n_blk // PLANES
    shape = (x, CORES, 2, PLANES // 2, y)
    wide = Mesh(np.asarray(mesh.devices).reshape(shape), AXES)
    split, gather = (("x", "zl", "y"), ()) if x * y * 2 <= 8 else (("x", "zl"), ("y",))
    spec = P(AXES, None, None)
    return jax.shard_map(
        functools.partial(shards, split, gather),
        mesh=wide,
        in_specs=(spec, spec, spec, P(), P()),
        out_specs=P(AXES, None),
        check_vma=False,
    )
```
